128 devices in a mesh: axial: 16 (over z, x), hoop: 8 (over y, core).
Axes of the slice: x: 4, y: 4, z: 4, core: 2. Of those that a mesh axis runs over, the one named last changes fastest.
Arguments:
- start_block: float32 [96, 3, 4, 16, 1024], P(None, None, None, 'axial', 'hoop'), may hold values from -8000 to 8000
- search_block: float32 [96, 3, 4, 16, 1024], P(None, None, None, 'axial', 'hoop'), may hold values from -8000 to 8000
- ritz_values: float32 [96], replicated, may hold values from 2 to 40
- element_matrix: float32 [24, 24], replicated, may hold values from -0.15 to 5, as said below
- moduli: float32 [3], replicated, may hold values from 0.5 to 4
- material_ids: int32 [3, 16, 1024], P(None, 'axial', 'hoop'), may hold values from 0 to 2
- held: int32 [4, 16, 1024], P(None, 'axial', 'hoop'), may hold values 0 or 1
Outputs:
- next_block: float32 [96, 3, 4, 16, 1024], P(None, None, None, 'axial', 'hoop')
- next_search: float32 [96, 3, 4, 16, 1024], P(None, None, None, 'axial', 'hoop')
The draws below stay inside these ranges and needn't reach their ends.
Inputs may be any that keep to these rules, and one draw needn't show every extreme that they name: `element_matrix`: symmetric; every diagonal entry exceeds the sum of the magnitudes of the other entries of its row.
All inputs are finite; a program needn't handle non-finite values. No bound on the sum of `held` on one device may be relied on, other than what follows from the above.
Results may differ from the reference program's by a relative error of at most 0.0003.
Values sent between devices are 32-bit elements; how exact they have to be, the bound alone decides.
A program may use at most 128 MiB of HBM per device.

```python
import math
import jax
import jax.numpy as jnp
from jax import lax

K = 96
ER = 3
MATS = 3
NAX = 16
NHOOP = 1024
DOFS = 196608


def shared_fields(key):
    key = jax.random.fold_in(key, 5)
    key_normal = jax.random.fold_in(key, 0)
    shape = (4, 3, ER + 1, NAX, NHOOP)
    drawn = jnp.clip(jax.random.normal(key_normal, shape, jnp.float32), -3.0, 3.0)
    return drawn


def scaled_block(key, shared, column_top):
    key_normal = jax.random.fold_in(key, 0)
    key_rows = jax.random.fold_in(key, 2)
    key_columns = jax.random.fold_in(key, 3)
    key_mixing = jax.random.fold_in(key, 4)
    shape = (K, 3, ER + 1, NAX, NHOOP)
    drawn = jnp.clip(jax.random.normal(key_normal, shape, jnp.float32), -4.0, 4.0)
    values = drawn
    mixing = jax.random.uniform(key_mixing, (K, 4), jnp.float32, -1.0, 1.0)
    for index in range(4):
        values = values + mixing[:, index][:, None, None, None, None] * shared[index][None]
    rows = jnp.exp(jax.random.uniform(key_rows, (ER + 1, NAX, NHOOP), jnp.float32, 0.0, math.log(10.0)))
    rise = 3.0 ** (lax.broadcasted_iota(jnp.float32, (1, NAX, 1), 1) / NAX)
    columns = jnp.exp(jax.random.uniform(key_columns, (K,), jnp.float32, 0.0, math.log(column_top)))
    return values * (rows * rise)[None, None] * columns[:, None, None, None, None]


def draw_start_block(key, part):
    column_top = 10.0
    shared = shared_fields(key)
    key = jax.random.fold_in(key, 11)
    return scaled_block(key, shared, column_top)


def draw_search_block(key, part):
    column_top = 10.0
    shared = shared_fields(key)
    key = jax.random.fold_in(key, 13)
    return scaled_block(key, shared, column_top)


def draw_element_matrix(key, part):
    key = jax.random.fold_in(key, 23)
    key_off, key_diag = jax.random.split(key, 2)
    off = jax.random.uniform(key_off, (24, 24), jnp.float32, -0.15, 0.15)
    off = 0.5 * (off + off.T)
    unit = jnp.eye(24, dtype=jnp.float32)
    diag = 4.0 + jax.random.uniform(key_diag, (24,), jnp.float32, 0.0, 1.0)
    return off * (1.0 - unit) + unit * diag[:, None]


def set_ends(array, stream_key, smallest, largest):
    shape = array.shape
    spot = [jax.random.randint(jax.random.fold_in(stream_key, axis), (), 0, shape[axis]) for axis in range(len(shape))]
    array = array.at[tuple(spot)].set(smallest)
    longest = shape.index(max(shape))
    spot[longest] = (spot[longest] + 1) % shape[longest]
    return array.at[tuple(spot)].set(largest)


def setup_inputs(seed: int = 0) -> dict:
    keys = jax.random.split(jax.random.key(seed), 8)
    start_block = draw_start_block(jax.random.fold_in(keys[7], 71), 0)
    search_block = draw_search_block(jax.random.fold_in(keys[7], 71), 0)
    ritz_values = jnp.clip(jnp.exp(jax.random.uniform(keys[2], (K,), jnp.float32, math.log(2.0), math.log(40.0))), 2.0, 40.0)
    element_matrix = draw_element_matrix(jax.random.fold_in(keys[7], 71), 0)
    moduli = jnp.clip(jnp.exp(jax.random.uniform(keys[4], (MATS,), jnp.float32, math.log(0.5), math.log(4.0))), 0.5, 4.0)
    material_ids = set_ends(jax.random.randint(keys[5], (ER, NAX, NHOOP), 0, MATS), jax.random.fold_in(keys[5], 1), 0, MATS - 1).astype(jnp.int32)
    held = set_ends((jax.random.randint(keys[6], (ER + 1, NAX, NHOOP), 0, 8) < 1).astype(jnp.int32), jax.random.fold_in(keys[6], 1), 0, 1)
    return {"start_block": start_block, "search_block": search_block, "ritz_values": ritz_values, "element_matrix": element_matrix, "moduli": moduli, "material_ids": material_ids, "held": held}


CORNERS = [(dr, da, dh) for dr in (0, 1) for da in (0, 1) for dh in (0, 1)]
shift_value = 1.0

def corner_products(ext, coef, kmat4, layers, along, around):
    corners = jnp.stack([ext[:, :, dr:dr + layers, da:da + along, dh:dh + around] for dr, da, dh in CORNERS], 0)
    parts = jnp.einsum('pqcd,ckdrah->pkqrah', kmat4, corners, precision=lax.Precision.HIGHEST)
    return parts * coef

def assemble(parts, shape, layers, along, around):
    total = jnp.zeros(shape, jnp.float32)
    for index, (dr, da, dh) in enumerate(CORNERS):
        total = total.at[:, :, dr:dr + layers, da:da + along, dh:dh + around].add(parts[index])
    return total

def operate(field, coef, kmat4, free):

    def one_block(block):
        ext = jnp.concatenate([block, block[..., :1]], 4)
        ext = jnp.concatenate([ext, jnp.zeros_like(ext[:, :, :, :1, :])], 3)
        parts = corner_products(ext, coef, kmat4, ER, NAX, NHOOP)
        total = assemble(parts, ext.shape, ER, NAX, NHOOP)
        total = total[:, :, :, :-1, :]
        total = total[..., :-1].at[..., :1].add(total[..., -1:])
        return total * free
    blocks = field.reshape((K // 8, 8) + field.shape[1:])
    return lax.map(one_block, blocks).reshape(field.shape)

def transposed_dot(left, right):
    return jnp.dot(left, right.T, precision=lax.Precision.HIGHEST)

def reference(start_block, search_block, ritz_values, element_matrix, moduli, material_ids, held):
    free = (1 - held).astype(jnp.float32)
    kmat4 = element_matrix.reshape(8, 3, 8, 3)
    coef = jnp.zeros(material_ids.shape, jnp.float32)
    for material in range(MATS):
        coef = coef + jnp.where(material_ids == material, moduli[material], jnp.float32(0.0))
    start_free = start_block * free
    search_free = search_block * free
    image_start = operate(start_free, coef, kmat4, free)
    image_search = operate(search_free, coef, kmat4, free)
    residual = image_start - ritz_values[:, None, None, None, None] * start_free
    image_residual = operate(residual, coef, kmat4, free)
    pieces = [start_free.reshape(K, -1), residual.reshape(K, -1), search_free.reshape(K, -1)]
    images = [image_start.reshape(K, -1), image_residual.reshape(K, -1), image_search.reshape(K, -1)]
    cross = jnp.block([[transposed_dot(left, right) for right in images] for left in pieces])
    gram_b = jnp.block([[transposed_dot(left, right) for right in pieces] for left in pieces])
    gram_a = 0.5 * (cross + cross.T)
    system = jnp.linalg.cholesky(gram_a + shift_value * gram_b)
    weights = jax.scipy.linalg.cho_solve((system, True), gram_b[:, :K])
    keep = (jnp.arange(3 * K) >= K).astype(jnp.float32)[:, None]
    weights_search = weights * keep
    small = jnp.dot(weights.T, jnp.dot(gram_b, weights, precision=lax.Precision.HIGHEST), precision=lax.Precision.HIGHEST)
    lower = jnp.linalg.cholesky(small)
    rotate = jax.scipy.linalg.solve_triangular(lower, weights.T, lower=True)
    rotate_search = jax.scipy.linalg.solve_triangular(lower, weights_search.T, lower=True)
    factor = jnp.sqrt(jnp.float32(DOFS))
    next_block = jnp.zeros((K, pieces[0].shape[1]), jnp.float32)
    next_search = jnp.zeros((K, pieces[0].shape[1]), jnp.float32)
    for index in range(3):
        next_block = next_block + jnp.dot(rotate[:, index * K:(index + 1) * K], pieces[index], precision=lax.Precision.HIGHEST)
        next_search = next_search + jnp.dot(rotate_search[:, index * K:(index + 1) * K], pieces[index], precision=lax.Precision.HIGHEST)
    return ((factor * next_block).reshape(start_block.shape), (factor * next_search).reshape(start_block.shape))
```

```python
import functools
import math

import jax
import jax.numpy as jnp
from jax import lax
from jax.experimental import pallas as pl
from jax.experimental.pallas import tpu as pltpu
from jax.sharding import PartitionSpec as P

HI = lax.Precision.HIGHEST
MESH = pl.DeviceIdType.MESH
K = 96
F32 = jnp.float32
BF16 = jnp.bfloat16
VMEM = pl.BlockSpec(memory_space=pltpu.VMEM)
SMEM = pl.BlockSpec(memory_space=pltpu.SMEM)
ROOM = 48 * 2**20
UNKNOWNS = 196608


def mm(a, b):
    return lax.dot_general(a, b, (((1,), (0,)), ((), ())), precision=HI, preferred_element_type=jnp.float32)

def mm_t(a, b):
    return lax.dot_general(a, b, (((0,), (0,)), ((), ())), precision=HI, preferred_element_type=jnp.float32)


def sweep(block, factor):
    lane = lax.broadcasted_iota(jnp.int32, (8, 128), 1)
    sub = lax.broadcasted_iota(jnp.int32, (8, 128), 0)
    tiles = [block[8 * t : 8 * t + 8, :] for t in range(12)]
    found = []
    for group in range(24):
        p = 4 * group
        home, low = p // 8, p % 8
        cols = [[jnp.broadcast_to(tile[:, p + j : p + j + 1], (8, 128)) for tile in tiles] for j in range(4)]
        rows = [jnp.broadcast_to(tiles[home][low + j : low + j + 1, :], (8, 128)) for j in range(4)]

        def entry(i, j):
            return jnp.broadcast_to(cols[j][home][low + i : low + i + 1, :], (8, 128))

        a00, a01, a11 = entry(0, 0), entry(0, 1), entry(1, 1)
        b00, b01, b10, b11 = entry(0, 2), entry(0, 3), entry(1, 2), entry(1, 3)
        c00, c01, c11 = entry(2, 2), entry(2, 3), entry(3, 3)
        ia = 1.0 / (a00 * a11 - a01 * a01)
        h00, h01, h11 = a11 * ia, -a01 * ia, a00 * ia
        x00, x01 = h00 * b00 + h01 * b10, h00 * b01 + h01 * b11
        x10, x11 = h01 * b00 + h11 * b10, h01 * b01 + h11 * b11
        s00 = c00 - (b00 * x00 + b10 * x10)
        s01 = c01 - (b00 * x01 + b10 * x11)
        s11 = c11 - (b01 * x01 + b11 * x11)
        ic = 1.0 / (s00 * s11 - s01 * s01)
        g00, g01, g11 = s11 * ic, -s01 * ic, s00 * ic
        picked = (lane >= p) & (lane < p + 4)
        full = [jnp.where(picked, jnp.where(lane == p + j, 1.0, 0.0), rows[j]) for j in range(4)]
        u0 = full[2] - (x00 * full[0] + x10 * full[1])
        u1 = full[3] - (x01 * full[0] + x11 * full[1])
        n2 = g00 * u0 + g01 * u1
        n3 = g01 * u0 + g11 * u1
        v0 = h00 * full[0] + h01 * full[1]
        v1 = h01 * full[0] + h11 * full[1]
        n0 = v0 - (x00 * n2 + x01 * n3)
        n1 = v1 - (x10 * n2 + x11 * n3)
        new = [n0, n1, n2, n3]
        if factor:
            left = [jnp.where(lane < p + 4, f, 0.0) for f in full]
            w0 = lax.rsqrt(a00)
            l0 = left[0] * w0
            e1 = a11 - a01 * a01 / a00
            l1 = (left[1] - (a01 / a00) * left[0]) * lax.rsqrt(e1)
            y0 = jnp.where(lane < p + 4, u0, 0.0)
            y1 = jnp.where(lane < p + 4, u1, 0.0)
            l2 = y0 * lax.rsqrt(s00)
            l3 = (y1 - (s01 / s00) * y0) * lax.rsqrt(s11 - s01 * s01 / s00)
            found.append([l0, l1, l2, l3])
        fresh = []
        for t, tile in enumerate(tiles):
            kept = jnp.where(picked, 0.0, tile)
            if t == home:
                here = (sub >= low) & (sub < low + 4)
                kept = jnp.where(here, 0.0, kept)
                q = [jnp.where(here, jnp.where(sub == low + j, -1.0, 0.0), cols[j][t]) for j in range(4)]
            else:
                q = [cols[j][t] for j in range(4)]
            fresh.append(kept - ((q[0] * n0 + q[1] * n1) + (q[2] * n2 + q[3] * n3)))
        tiles = fresh
    if factor:
        out = []
        for t in range(12):
            eight = found[2 * t] + found[2 * t + 1]
            tile = eight[0]
            for s in range(1, 8):
                tile = jnp.where(sub == s, eight[s], tile)
            out.append(tile)
        return jnp.concatenate(out, 0)
    return jnp.concatenate(tiles, 0)


def diagonal(block):
    lane = lax.broadcasted_iota(jnp.int32, (K, 128), 1)
    row = lax.broadcasted_iota(jnp.int32, (K, 128), 0)
    only = jnp.where(lane == row, block, 0.0)
    down = jnp.sum(only, 1, keepdims=True)
    along = jnp.sum(only, 0, keepdims=True)
    return lax.rsqrt(down), lax.rsqrt(jnp.where(along == 0.0, 1.0, along))


def cut(block):
    return block[:, :K]


def pad(block):
    return jnp.concatenate([block, jnp.zeros((block.shape[0], 128 - block.shape[1]), jnp.float32)], 1)


def rotation(gram, scale, rot_ref):
    b = [gram[i] for i in range(6)]
    a = [gram[6 + i] for i in range(6)]
    m = [x + y for x, y in zip(a, b)]
    d0, e0 = diagonal(m[0])
    d1, e1 = diagonal(m[3])
    d2, e2 = diagonal(m[5])
    m11, m12, m13 = m[0] * d0 * e0, m[1] * d0 * e1, m[2] * d0 * e2
    m22, m23, m33 = m[3] * d1 * e1, m[4] * d1 * e2, m[5] * d2 * e2
    bsr_t, bsp_t, brp_t = (pad(cut(x).T) for x in (b[1], b[2], b[4]))
    f1, f2, f3 = b[0] * d0, bsr_t * d1, bsp_t * d2
    i1 = sweep(m11, False)
    t1 = mm(cut(i1), jnp.concatenate([m12, m13, f1], 1))
    t12, t13, y1 = t1[:, :128], t1[:, 128:256], t1[:, 256:]
    s2 = jnp.concatenate([m22, m23, f2], 1) - mm(cut(m12).T, t1)
    s3 = jnp.concatenate([m33, f3], 1) - mm(cut(m13).T, t1[:, 128:])
    i2 = sweep(s2[:, :128], False)
    m23 = s2[:, 128:256]
    t2 = mm(cut(i2), s2[:, 128:])
    s3 = s3 - mm(cut(m23).T, t2)
    i3 = sweep(s3[:, :128], False)
    w3 = mm(cut(i3), s3[:, 128:])
    w2 = t2[:, 128:] - mm(cut(t2), w3)
    w1 = y1 - mm(jnp.concatenate([cut(t12), cut(t13)], 1), jnp.concatenate([w2, w3], 0))
    w = jnp.concatenate([w1 * d0, w2 * d1, w3 * d2], 0)
    big = jnp.concatenate(
        [
            jnp.concatenate([cut(b[0]), cut(b[1]), cut(b[2])], 1),
            jnp.concatenate([cut(bsr_t), cut(b[3]), cut(b[4])], 1),
            jnp.concatenate([cut(bsp_t), cut(brp_t), cut(b[5])], 1),
        ],
        0,
    )
    wt = cut(w).T
    small = mm(wt, mm(big, w))
    ds, es = diagonal(small)
    inv = sweep(small * ds * es, True) * es
    rot_ref[...] = mm(cut(inv), wt) * scale


def mm_nt(a, b):
    return lax.dot_general(a, b, (((1,), (1,)), ((), ())), precision=HI, preferred_element_type=F32)


def call(kernel, shapes, count, scratch=(), memory=None, name=None):
    return pl.pallas_call(
        kernel,
        out_shape=[jax.ShapeDtypeStruct(*shape) for shape in shapes],
        in_specs=memory or [VMEM] * count,
        out_specs=[VMEM] * len(shapes),
        scratch_shapes=list(scratch),
        compiler_params=pltpu.CompilerParams(vmem_limit_bytes=ROOM),
        name=name,
    )


def split(x):
    high = x.astype(BF16)
    rest = x - high.astype(F32)
    middle = rest.astype(BF16)
    low = (rest - middle.astype(F32)).astype(BF16)
    return high, middle, low


def stencil(kmat):
    def rows_of(shape, axis):
        at = lax.broadcasted_iota(jnp.int32, shape, axis)
        low, high = at % 8, at // 8
        dh, high = high % 2, high // 2
        return low // 3, low % 3, dh, high % 3, high // 3, low < 6

    def columns_of(shape, axis):
        at = lax.broadcasted_iota(jnp.int32, shape, axis)
        low, high = at % 8, at // 8
        return low // 3, low % 3, high // 4, high % 4, low < 6

    da, q, dh, _, dr, real = rows_of((96, 24), 0)
    corner = lax.broadcasted_iota(jnp.int32, (96, 24), 1)
    pick = jnp.where(real & (corner == 3 * (4 * dr + 2 * da + dh) + q), 1.0, 0.0)
    picked = mm(pick, kmat)
    layer = rows_of((96, 64), 0)[3]
    node = columns_of((96, 64), 1)[3]
    total = jnp.zeros((96, 64), F32)
    for dr in range(2):
        da, q, dh, _, real = columns_of((24, 64), 1)
        corner = lax.broadcasted_iota(jnp.int32, (24, 64), 0)
        place = jnp.where(real & (corner == 3 * (4 * dr + 2 * da + dh) + q), 1.0, 0.0)
        total = total + jnp.where(node == layer + dr, mm(picked, place), 0.0)
    high, middle, low = split(total)
    return jnp.concatenate([high, high, high, middle, middle, low], 1)


def put(field_ref, near, far, near_edge, far_edge):
    lane = lax.broadcasted_iota(jnp.int32, (K, 128), 1)
    zero = jnp.zeros((K, 128), F32)
    for high in range(8):
        for low in (6, 7):
            field_ref[pl.ds(8 * high + low, K, stride=64), :] = zero
    for da, (field, edge) in enumerate(((near, near_edge), (far, far_edge))):
        edge = edge[...]
        for q in range(3):
            for r in range(4):
                i = 4 * q + r
                tile = field[:, 128 * i : 128 * i + 128]
                field_ref[pl.ds(8 * r + 3 * da + q, K, stride=64), :] = tile
                moved = jnp.where(lane == 127, pltpu.roll(edge, 127 - i, 1), pltpu.roll(tile, 127, 1))
                field_ref[pl.ds(32 + 8 * r + 3 * da + q, K, stride=64), :] = moved


def products(field_ref, image_ref, stencil_ref, coef):
    weights = stencil_ref[...]
    coef = [jnp.broadcast_to(coef[r : r + 1], (8, 128)) for r in range(3)]

    def step(pair, carry):
        base = pl.multiple_of(128 * pair, 128)
        both = field_ref[pl.ds(base, 128), :]
        high, middle, low = split(jnp.concatenate([both[:64], both[64:]], 1))
        stack = jnp.concatenate([high, middle, low, high, middle, high], 0)
        terms = jnp.dot(weights, stack, preferred_element_type=F32)
        for half in range(2):
            term = terms[:, 128 * half : 128 * half + 128]

            def part(dr, r, dh):
                at = 8 * ((dr * 3 + r) * 2 + dh)
                return term[at : at + 8] * coef[r]

            for dh in range(2):
                for node in range(4):
                    parts = [part(dr, node - dr, dh) for dr in range(2) if 0 <= node - dr < 3]
                    value = parts[0] if len(parts) == 1 else parts[0] + parts[1]
                    image_ref[pl.ds(base + 64 * half + 32 * dh + 8 * node, 8), :] = value
        return carry

    lax.fori_loop(0, K // 2, step, 0, unroll=2)


def take(image_ref, da, store):
    lane = lax.broadcasted_iota(jnp.int32, (K, 128), 1)
    over = jnp.zeros((K, 128), F32)
    for q in range(3):
        for r in range(4):
            i = 4 * q + r
            at = 8 * r + 3 * da + q
            first = image_ref[pl.ds(at, K, stride=64), :]
            second = pltpu.roll(image_ref[pl.ds(32 + at, K, stride=64), :], 1, 1)
            store(i, first + jnp.where(lane == 0, 0.0, second))
            over = jnp.where(lane == i, pltpu.roll(second, i, 1), over)
    return over


def coefficients(ids_ref, moduli_ref):
    ids = ids_ref[...]
    coef = jnp.zeros(ids.shape, F32)
    for material in range(3):
        coef = coef + jnp.where(ids == material, moduli_ref[material], 0.0)
    return coef


def load_kernel(start_ref, search_ref, held_ref, kmat_ref, s_ref, p_ref, s_edge_ref, p_edge_ref, stencil_ref):
    free = (1 - held_ref[...]).astype(F32)
    lane = lax.broadcasted_iota(jnp.int32, (K, 128), 1)
    for source, field, edge_ref in ((start_ref, s_ref, s_edge_ref), (search_ref, p_ref, p_edge_ref)):
        edge = jnp.zeros((K, 128), F32)
        for i in range(12):
            tile = source[pl.ds(i, K, stride=12), :] * free[i % 4 : i % 4 + 1]
            field[:, 128 * i : 128 * i + 128] = tile
            edge = jnp.where(lane == i, pltpu.roll(tile, i, 1) if i else tile, edge)
        edge_ref[...] = edge
    stencil_ref[...] = stencil(kmat_ref[...])


def image_kernel(
    s_ref, far_ref, edge_ref, far_edge_ref, ids_ref, stencil_ref, moduli_ref,
    near_ref, next_ref, over_ref, next_over_ref, field, image,
):
    put(field, s_ref, far_ref, edge_ref, far_edge_ref)
    products(field, image, stencil_ref, coefficients(ids_ref, moduli_ref))
    for da, (target, over) in enumerate(((near_ref, over_ref), (next_ref, next_over_ref))):

        def store(i, value, target=target):
            target[:, 128 * i : 128 * i + 128] = value

        over[...] = take(image, da, store)


def residual_kernel(s_ref, near_ref, below_ref, over_ref, below_over_ref, held_ref, ritz_ref, image_ref, r_ref, edge_ref):
    free = (1 - held_ref[...]).astype(F32)
    lane = lax.broadcasted_iota(jnp.int32, (K, 128), 1)
    over = over_ref[...] + below_over_ref[...]
    edge = jnp.zeros((K, 128), F32)
    for i in range(12):
        lanes = slice(128 * i, 128 * i + 128)
        came = jnp.where(lane == 0, pltpu.roll(over, 128 - i, 1) if i else over, 0.0)
        image = (near_ref[:, lanes] + below_ref[:, lanes] + came) * free[i % 4 : i % 4 + 1]
        tile = image - ritz_ref[...] * s_ref[:, lanes]
        image_ref[:, lanes] = image
        r_ref[:, lanes] = tile
        edge = jnp.where(lane == i, pltpu.roll(tile, i, 1) if i else tile, edge)
    edge_ref[...] = edge


def gram_kernel(
    s_ref, image_ref, r_ref, r_far_ref, r_edge_ref, r_far_edge_ref, p_ref, p_far_ref, p_edge_ref, p_far_edge_ref,
    ids_ref, stencil_ref, moduli_ref, gram_ref, field, image, wide,
):
    coef = coefficients(ids_ref, moduli_ref)
    blocks = [None] * 12
    s, r, p = s_ref[...], r_ref[...], p_ref[...]
    rows = jnp.concatenate([s, r, p], 0)
    b_s, b_r, b_p = mm_nt(s, rows), mm_nt(r, rows[K:]), mm_nt(p, p)
    a_s = mm_nt(image_ref[...], rows)
    wholes = []
    for near, far, edge, far_edge in (
        (r_ref, r_far_ref, r_edge_ref, r_far_edge_ref),
        (p_ref, p_far_ref, p_edge_ref, p_far_edge_ref),
    ):
        wholes.append(jnp.concatenate([near[...], far[...], edge[...], far_edge[...]], 1))
        put(field, near, far, edge, far_edge)
        products(field, image, stencil_ref, coef)
        for da in range(2):

            def store(i, value, da=da):
                wide[:, 1536 * da + 128 * i : 1536 * da + 128 * i + 128] = value

            wide[:, 3072 + 128 * da : 3200 + 128 * da] = take(image, da, store)
        if len(wholes) == 1:
            a_r_r = mm_nt(wide[...], wholes[0])
            whole = jnp.concatenate([p_ref[...], p_far_ref[...], p_edge_ref[...], p_far_edge_ref[...]], 1)
            a_r_p = mm_nt(wide[...], whole)
        else:
            a_p_p = mm_nt(wide[...], wholes[1])
    blocks = [b_s[:, :K], b_s[:, K : 2 * K], b_s[:, 2 * K :], b_r[:, :K], b_r[:, K:], b_p]
    blocks += [a_s[:, :K], a_s[:, K : 2 * K], a_s[:, 2 * K :], a_r_r, a_r_p, a_p_p]
    blocks = [pad(block) for block in blocks]
    lane = lax.broadcasted_iota(jnp.int32, (K, 128), 1)
    for group in range(3):
        for j in range(3):
            extra = pltpu.roll(blocks[9 + group], 96 - 32 * j, 1)
            whole = jnp.where(lane < K, blocks[3 * group + j], extra)
            gram_ref[12 * (3 * group + j) : 12 * (3 * group + j) + 12] = whole.reshape(12, 8, 128)
    gram_ref[108:128] = jnp.zeros((20, 8, 128), F32)


def unpack(gram_ref):
    lane = lax.broadcasted_iota(jnp.int32, (K, 128), 1)
    blocks = [None] * 12
    for group in range(3):
        extra = jnp.zeros((K, 128), F32)
        for j in range(3):
            whole = gram_ref[12 * (3 * group + j) : 12 * (3 * group + j) + 12].reshape(K, 128)
            blocks[3 * group + j] = jnp.where(lane < K, whole, 0.0)
            here = (lane >= 32 * j) & (lane < 32 * j + 32)
            extra = jnp.where(here, pltpu.roll(whole, 32 + 32 * j, 1), extra)
        blocks[9 + group] = extra
    return blocks


def sum_kernel(g_ref, out_ref, from_core, half, from_x, quarter, from_y, from_z, send, recv):
    axial, hoop = lax.axis_index("axial"), lax.axis_index("hoop")
    z, x = axial // 4, axial % 4
    y, core = hoop // 2, hoop % 2

    def at(z, x, y, core):
        return (z * 4 + x, y * 2 + core)

    def others(axis):
        if axis == "core":
            return [at(z, x, y, 1 - core)]
        turn = [lambda v, d: (v + d) % 4]
        if axis == "x":
            return [at(z, (x + d) % 4, y, core) for d in (1, 2, 3)]
        if axis == "y":
            return [at(z, x, (y + d) % 4, core) for d in (1, 2, 3)]
        return [at((z + d) % 4, x, y, core) for d in (1, 2, 3)]

    barrier = pltpu.get_barrier_semaphore()
    for axis in ("core", "x", "y", "z"):
        for peer in others(axis):
            pl.semaphore_signal(barrier, inc=1, device_id=peer, device_id_type=MESH)
    pl.semaphore_wait(barrier, 10)
    used = [0]

    def copy(source, target, peer):
        index = used[0]
        used[0] += 1
        made = pltpu.make_async_remote_copy(
            src_ref=source, dst_ref=target, send_sem=send.at[index], recv_sem=recv.at[index],
            device_id=peer, device_id_type=MESH,
        )
        made.start()
        return made

    def finish(copies):
        for made in copies:
            made.wait()

    finish([copy(g_ref.at[pl.ds((1 - core) * 64, 64)], from_core, others("core")[0])])
    half[...] = g_ref[pl.ds(core * 64, 64)] + from_core[...]
    finish(
        [
            copy(half.at[pl.ds(((x + d) % 4) * 16, 16)], from_x.at[d - 1], others("x")[d - 1])
            for d in (1, 2, 3)
        ]
    )
    quarter[...] = (half[pl.ds(x * 16, 16)] + from_x[0]) + (from_x[1] + from_x[2])
    finish(
        [
            copy(quarter.at[pl.ds(((y + d) % 4) * 4, 4)], from_y.at[d - 1], others("y")[d - 1])
            for d in (1, 2, 3)
        ]
    )
    from_z[z] = (quarter[pl.ds(y * 4, 4)] + from_y[0]) + (from_y[1] + from_y[2])
    finish([copy(from_z.at[z], from_z.at[z], peer) for peer in others("z")])
    base = core * 64 + x * 16 + y * 4
    out_ref[pl.ds(base, 4)] = (from_z[0] + from_z[1]) + (from_z[2] + from_z[3])
    for axis, first, size in (("y", base, 4), ("x", core * 64 + x * 16, 16), ("core", core * 64, 64)):
        part = out_ref.at[pl.ds(first, size)]
        finish([copy(part, part, peer) for peer in others(axis)])


def sum_over_devices(gram):
    def tiles(*shape):
        return pltpu.VMEM(shape + (8, 128), F32)

    return pl.pallas_call(
        sum_kernel,
        out_shape=jax.ShapeDtypeStruct((128, 8, 128), F32),
        in_specs=[VMEM],
        out_specs=VMEM,
        scratch_shapes=[
            tiles(64), tiles(64), tiles(3, 16), tiles(16), tiles(3, 4), tiles(4, 4),
            pltpu.SemaphoreType.DMA((17,)), pltpu.SemaphoreType.DMA((17,)),
        ],
        compiler_params=pltpu.CompilerParams(vmem_limit_bytes=ROOM, collective_id=0, has_side_effects=True),
        name="gram_sum",
    )(gram)


def dense_kernel(gram_ref, s_ref, r_ref, p_ref, block_ref, search_ref, rot_ref):
    rotation(unpack(gram_ref), math.sqrt(UNKNOWNS), rot_ref)
    rot = rot_ref[...]
    for i in range(6):
        lanes = slice(256 * i, 256 * i + 256)
        tail = mm(rot[:, K:], jnp.concatenate([r_ref[:, lanes], p_ref[:, lanes]], 0))
        head = tail + mm(rot[:, :K], s_ref[:, lanes])
        for h in range(2):
            block_ref[pl.ds(2 * i + h, K, stride=12), :] = head[:, 128 * h : 128 * h + 128]
            search_ref[pl.ds(2 * i + h, K, stride=12), :] = tail[:, 128 * h : 128 * h + 128]


def shifted(block, axes, by):
    counts = [lax.axis_size(axis) for axis in ("axial", "hoop")]
    pairs = []
    for axial in range(counts[0]):
        for hoop in range(counts[1]):
            to_axial = axial + (by if "axial" in axes else 0)
            to_hoop = (hoop + (by if "hoop" in axes else 0)) % counts[1]
            if 0 <= to_axial < counts[0]:
                pairs.append((axial * counts[1] + hoop, to_axial * counts[1] + to_hoop))
    return lax.ppermute(block, ("axial", "hoop"), pairs)


def on_device(start_block, search_block, ritz_values, element_matrix, moduli, material_ids, held):
    shape = start_block.shape
    field, edge = ((K, 1536), F32), ((K, 128), F32)
    columns = [pltpu.VMEM((K * 64, 128), F32)] * 2
    start, search = start_block.reshape(1152, 128), search_block.reshape(1152, 128)
    held, ids = held.reshape(4, 128), material_ids.reshape(3, 128)
    s, p, s_edge, p_edge, weights = call(load_kernel, [field, field, edge, edge, ((96, 384), BF16)], 4, name="load")(
        start, search, held, element_matrix
    )

    def around(x, x_edge):
        return shifted(x, ("axial",), -1), shifted(x_edge, ("hoop",), -1), shifted(x_edge, ("axial", "hoop"), -1)

    s_around = around(s, s_edge)
    p_around = around(p, p_edge)
    near, after, over, after_over = call(
        image_kernel, [field, field, edge, edge], 7, columns, [VMEM] * 6 + [SMEM], name="image"
    )(s, *s_around, ids, weights, moduli)
    below = shifted(after, ("axial",), 1)
    left = shifted(over, ("hoop",), 1)
    below_left = shifted(after_over, ("axial", "hoop"), 1)
    image, r, r_edge = call(residual_kernel, [field, field, edge], 7, name="residual")(
        s, near, below, left, below_left, held, ritz_values.reshape(K, 1)
    )
    r_around = around(r, r_edge)
    gram = call(
        gram_kernel,
        [((128, 8, 128), F32)],
        13,
        columns + [pltpu.VMEM((K, 3328), F32)],
        [VMEM] * 12 + [SMEM],
        name="gram",
    )(s, image, r, *r_around, p, *p_around, ids, weights, moduli)[0]
    gram = sum_over_devices(gram)
    out = ((1152, 128), F32)
    block, search = call(dense_kernel, [out, out], 4, [pltpu.VMEM((K, 288), F32)], name="dense")(gram, s, r, p)
    return block.reshape(shape), search.reshape(shape)


def solution(mesh):
    split_field = P(None, None, None, "axial", "hoop")
    split_nodes = P(None, "axial", "hoop")
    in_specs = (split_field, split_field, P(), P(), P(), split_nodes, split_nodes)
    return jax.shard_map(
        on_device, mesh=mesh, in_specs=in_specs, out_specs=(split_field, split_field), check_vma=False
    )
```

```python
import functools
import math

import jax
import jax.numpy as jnp
from jax import lax
from jax.experimental import pallas as pl
from jax.experimental.pallas import tpu as pltpu
from jax.sharding import PartitionSpec as P

HI = lax.Precision.HIGHEST
MESH = pl.DeviceIdType.MESH
K = 96
F32 = jnp.float32
BF16 = jnp.bfloat16
VMEM = pl.BlockSpec(memory_space=pltpu.VMEM)
SMEM = pl.BlockSpec(memory_space=pltpu.SMEM)
ROOM = 48 * 2**20
UNKNOWNS = 196608
UNROLL = 2
COPIES = 38


def mm(a, b):
    return lax.dot_general(a, b, (((1,), (0,)), ((), ())), precision=HI, preferred_element_type=jnp.float32)

def mm_t(a, b):
    return lax.dot_general(a, b, (((0,), (0,)), ((), ())), precision=HI, preferred_element_type=jnp.float32)


def sweep(block, factor):
    lane = lax.broadcasted_iota(jnp.int32, (8, 128), 1)
    sub = lax.broadcasted_iota(jnp.int32, (8, 128), 0)
    tiles = [block[8 * t : 8 * t + 8, :] for t in range(12)]
    found = []
    for group in range(24):
        p = 4 * group
        home, low = p // 8, p % 8
        cols = [[jnp.broadcast_to(tile[:, p + j : p + j + 1], (8, 128)) for tile in tiles] for j in range(4)]
        rows = [jnp.broadcast_to(tiles[home][low + j : low + j + 1, :], (8, 128)) for j in range(4)]

        def entry(i, j):
            return jnp.broadcast_to(cols[j][home][low + i : low + i + 1, :], (8, 128))

        a00, a01, a11 = entry(0, 0), entry(0, 1), entry(1, 1)
        b00, b01, b10, b11 = entry(0, 2), entry(0, 3), entry(1, 2), entry(1, 3)
        c00, c01, c11 = entry(2, 2), entry(2, 3), entry(3, 3)
        ia = 1.0 / (a00 * a11 - a01 * a01)
        h00, h01, h11 = a11 * ia, -a01 * ia, a00 * ia
        x00, x01 = h00 * b00 + h01 * b10, h00 * b01 + h01 * b11
        x10, x11 = h01 * b00 + h11 * b10, h01 * b01 + h11 * b11
        s00 = c00 - (b00 * x00 + b10 * x10)
        s01 = c01 - (b00 * x01 + b10 * x11)
        s11 = c11 - (b01 * x01 + b11 * x11)
        ic = 1.0 / (s00 * s11 - s01 * s01)
        g00, g01, g11 = s11 * ic, -s01 * ic, s00 * ic
        picked = (lane >= p) & (lane < p + 4)
        full = [jnp.where(picked, jnp.where(lane == p + j, 1.0, 0.0), rows[j]) for j in range(4)]
        u0 = full[2] - (x00 * full[0] + x10 * full[1])
        u1 = full[3] - (x01 * full[0] + x11 * full[1])
        n2 = g00 * u0 + g01 * u1
        n3 = g01 * u0 + g11 * u1
        v0 = h00 * full[0] + h01 * full[1]
        v1 = h01 * full[0] + h11 * full[1]
        n0 = v0 - (x00 * n2 + x01 * n3)
        n1 = v1 - (x10 * n2 + x11 * n3)
        new = [n0, n1, n2, n3]
        if factor:
            left = [jnp.where(lane < p + 4, f, 0.0) for f in full]
            w0 = lax.rsqrt(a00)
            l0 = left[0] * w0
            e1 = a11 - a01 * a01 / a00
            l1 = (left[1] - (a01 / a00) * left[0]) * lax.rsqrt(e1)
            y0 = jnp.where(lane < p + 4, u0, 0.0)
            y1 = jnp.where(lane < p + 4, u1, 0.0)
            l2 = y0 * lax.rsqrt(s00)
            l3 = (y1 - (s01 / s00) * y0) * lax.rsqrt(s11 - s01 * s01 / s00)
            found.append([l0, l1, l2, l3])
        fresh = []
        for t, tile in enumerate(tiles):
            kept = jnp.where(picked, 0.0, tile)
            if t == home:
                here = (sub >= low) & (sub < low + 4)
                kept = jnp.where(here, 0.0, kept)
                q = [jnp.where(here, jnp.where(sub == low + j, -1.0, 0.0), cols[j][t]) for j in range(4)]
            else:
                q = [cols[j][t] for j in range(4)]
            fresh.append(kept - ((q[0] * n0 + q[1] * n1) + (q[2] * n2 + q[3] * n3)))
        tiles = fresh
    if factor:
        out = []
        for t in range(12):
            eight = found[2 * t] + found[2 * t + 1]
            tile = eight[0]
            for s in range(1, 8):
                tile = jnp.where(sub == s, eight[s], tile)
            out.append(tile)
        return jnp.concatenate(out, 0)
    return jnp.concatenate(tiles, 0)


def diagonal(block):
    lane = lax.broadcasted_iota(jnp.int32, (K, 128), 1)
    row = lax.broadcasted_iota(jnp.int32, (K, 128), 0)
    only = jnp.where(lane == row, block, 0.0)
    down = jnp.sum(only, 1, keepdims=True)
    along = jnp.sum(only, 0, keepdims=True)
    return lax.rsqrt(down), lax.rsqrt(jnp.where(along == 0.0, 1.0, along))


def cut(block):
    return block[:, :K]


def pad(block):
    return jnp.concatenate([block, jnp.zeros((block.shape[0], 128 - block.shape[1]), jnp.float32)], 1)


def rotation(gram, scale, rot_ref):
    b = [gram[i] for i in range(6)]
    a = [gram[6 + i] for i in range(6)]
    m = [x + y for x, y in zip(a, b)]
    d0, e0 = diagonal(m[0])
    d1, e1 = diagonal(m[3])
    d2, e2 = diagonal(m[5])
    m11, m12, m13 = m[0] * d0 * e0, m[1] * d0 * e1, m[2] * d0 * e2
    m22, m23, m33 = m[3] * d1 * e1, m[4] * d1 * e2, m[5] * d2 * e2
    bsr_t, bsp_t, brp_t = (pad(cut(x).T) for x in (b[1], b[2], b[4]))
    f1, f2, f3 = b[0] * d0, bsr_t * d1, bsp_t * d2
    i1 = sweep(m11, False)
    t1 = mm(cut(i1), jnp.concatenate([m12, m13, f1], 1))
    t12, t13, y1 = t1[:, :128], t1[:, 128:256], t1[:, 256:]
    s2 = jnp.concatenate([m22, m23, f2], 1) - mm(cut(m12).T, t1)
    s3 = jnp.concatenate([m33, f3], 1) - mm(cut(m13).T, t1[:, 128:])
    i2 = sweep(s2[:, :128], False)
    m23 = s2[:, 128:256]
    t2 = mm(cut(i2), s2[:, 128:])
    s3 = s3 - mm(cut(m23).T, t2)
    i3 = sweep(s3[:, :128], False)
    w3 = mm(cut(i3), s3[:, 128:])
    w2 = t2[:, 128:] - mm(cut(t2), w3)
    w1 = y1 - mm(jnp.concatenate([cut(t12), cut(t13)], 1), jnp.concatenate([w2, w3], 0))
    w = jnp.concatenate([w1 * d0, w2 * d1, w3 * d2], 0)
    big = jnp.concatenate(
        [
            jnp.concatenate([cut(b[0]), cut(b[1]), cut(b[2])], 1),
            jnp.concatenate([cut(bsr_t), cut(b[3]), cut(b[4])], 1),
            jnp.concatenate([cut(bsp_t), cut(brp_t), cut(b[5])], 1),
        ],
        0,
    )
    wt = cut(w).T
    small = mm(wt, mm(big, w))
    ds, es = diagonal(small)
    inv = sweep(small * ds * es, True) * es
    rot_ref[...] = mm(cut(inv), wt) * scale


def mm_nt(a, b):
    return lax.dot_general(a, b, (((1,), (1,)), ((), ())), precision=HI, preferred_element_type=F32)


def split(x):
    high = x.astype(BF16)
    rest = x - high.astype(F32)
    middle = rest.astype(BF16)
    low = (rest - middle.astype(F32)).astype(BF16)
    return high, middle, low


def stencil(kmat):
    def rows_of(shape, axis):
        at = lax.broadcasted_iota(jnp.int32, shape, axis)
        low, high = at % 8, at // 8
        dh, high = high % 2, high // 2
        return low // 3, low % 3, dh, high % 3, high // 3, low < 6

    def columns_of(shape, axis):
        at = lax.broadcasted_iota(jnp.int32, shape, axis)
        low, high = at % 8, at // 8
        return low // 3, low % 3, high // 4, high % 4, low < 6

    da, q, dh, _, dr, real = rows_of((96, 24), 0)
    corner = lax.broadcasted_iota(jnp.int32, (96, 24), 1)
    pick = jnp.where(real & (corner == 3 * (4 * dr + 2 * da + dh) + q), 1.0, 0.0)
    picked = mm(pick, kmat)
    layer = rows_of((96, 64), 0)[3]
    node = columns_of((96, 64), 1)[3]
    total = jnp.zeros((96, 64), F32)
    for dr in range(2):
        da, q, dh, _, real = columns_of((24, 64), 1)
        corner = lax.broadcasted_iota(jnp.int32, (24, 64), 0)
        place = jnp.where(real & (corner == 3 * (4 * dr + 2 * da + dh) + q), 1.0, 0.0)
        total = total + jnp.where(node == layer + dr, mm(picked, place), 0.0)
    high, middle, low = split(total)
    return jnp.concatenate([high, high, high, middle, middle, low], 1)


def lanes_of(rows):
    return lax.broadcasted_iota(jnp.int32, (rows, 128), 1)


def turn(x, by):
    return pltpu.roll(x, by % 128, 1) if by % 128 else x


def swap(tiles):
    lane = lanes_of(tiles[0].shape[0])
    front, even = lane < 64, (lane // 32) % 2 == 0
    a, b, c, d = tiles
    a, c = jnp.where(front, a, turn(c, 64)), jnp.where(front, turn(a, 64), c)
    b, d = jnp.where(front, b, turn(d, 64)), jnp.where(front, turn(b, 64), d)
    a, b = jnp.where(even, a, turn(b, 32)), jnp.where(even, turn(a, 96), b)
    c, d = jnp.where(even, c, turn(d, 32)), jnp.where(even, turn(c, 96), d)
    return a, b, c, d


def tile(ref, i):
    return ref[:, 128 * i : 128 * i + 128]


def set_tile(ref, i, value):
    ref[:, 128 * i : 128 * i + 128] = value


def pack(field_ref, pack_ref):
    for q in range(3):
        for to, value in enumerate(swap([tile(field_ref, 4 * q + r) for r in range(4)])):
            pack_ref[to, 96 * q : 96 * q + 96, :] = value


def unpack(came_ref, field_ref):
    for q in range(3):
        for r, value in enumerate(swap([came_ref[j, 96 * q : 96 * q + 96, :] for j in range(4)])):
            set_tile(field_ref, 4 * q + r, value)


def first_nodes(field_ref, layer_ref, edge_ref):
    lane = lanes_of(K)
    edge = jnp.zeros((K, 128), F32)
    for q in range(3):
        layer = jnp.zeros((K, 128), F32)
        for r in range(4):
            value = tile(field_ref, 4 * q + r)
            layer = jnp.where(lane // 32 == r, turn(value, 32 * r), layer)
            edge = jnp.where(lane % 32 == 4 * q + r, turn(value, 4 * q + r), edge)
        layer_ref[96 * q : 96 * q + 96, :] = layer
    edge_ref[...] = edge


def put(columns_ref, field_ref, layer_ref, edge, far_edge, top):
    lane = lanes_of(K)
    for q in range(3):
        for r in range(4):
            i = 4 * q + r
            near = tile(field_ref, i)
            ahead = jnp.where(top, 0.0, turn(layer_ref[96 * q : 96 * q + 96, :], 32 * (3 - r)))
            far = jnp.where(lane < 96, turn(near, 96), ahead)
            for da, (value, side) in enumerate(((near, edge), (far, far_edge))):
                at = 8 * r + 3 * da + q
                columns_ref[pl.ds(at, K, stride=64), :] = value
                moved = jnp.where(lane % 32 == 31, turn(side, 31 - i), turn(value, 127))
                columns_ref[pl.ds(32 + at, K, stride=64), :] = moved


def far_edges(edge, corner, top):
    lane = lanes_of(K)
    corner = jnp.where(top, 0.0, jnp.where(lane < 96, 0.0, turn(corner, 96)))
    return corner, jnp.where(lane < 96, turn(edge, 96), corner)


def products(columns_ref, image_ref, stencil_ref, coef):
    weights = stencil_ref[...]
    coef = [jnp.broadcast_to(coef[r : r + 1], (8, 128)) for r in range(3)]
    wide = 8

    def step(group, carry):
        base = pl.multiple_of(64 * wide * group, 64 * wide)
        some = columns_ref[pl.ds(base, 64 * wide), :]
        high, middle, low = split(jnp.concatenate([some[64 * c : 64 * c + 64] for c in range(wide)], 1))
        stack = jnp.concatenate([high, middle, low, high, middle, high], 0)
        terms = jnp.dot(weights, stack, preferred_element_type=F32)
        for c in range(wide):
            term = terms[:, 128 * c : 128 * c + 128]

            def part(dr, r, dh):
                at = 8 * ((dr * 3 + r) * 2 + dh)
                return term[at : at + 8] * coef[r]

            values = []
            for dh in range(2):
                for node in range(4):
                    parts = [part(dr, node - dr, dh) for dr in range(2) if 0 <= node - dr < 3]
                    values.append(parts[0] if len(parts) == 1 else parts[0] + parts[1])
            image_ref[pl.ds(base + 64 * c, 64), :] = jnp.concatenate(values, 0)
        return carry

    lax.fori_loop(0, K // wide, step, 0, unroll=UNROLL)


def take(image_ref, wide_ref):
    lane = lanes_of(K)
    over, far_over = jnp.zeros((K, 128), F32), jnp.zeros((K, 128), F32)
    for q in range(3):
        layer = jnp.zeros((K, 128), F32)
        for r in range(4):
            i = 4 * q + r
            at = 8 * r + q

            def shifted_sum(at):
                second = image_ref[pl.ds(32 + at, K, stride=64), :]
                first = image_ref[pl.ds(at, K, stride=64), :]
                return first + jnp.where(lane % 32 == 0, 0.0, turn(second, 1)), turn(second, i - 31)

            near, out = shifted_sum(at)
            far, far_out = shifted_sum(at + 3)
            over = jnp.where(lane % 32 == i, out, over)
            far_over = jnp.where(lane % 32 == i, far_out, far_over)
            set_tile(wide_ref, i, near + jnp.where(lane < 32, 0.0, turn(far, 32)))
            layer = jnp.where(lane // 32 == r, turn(far, 32 * (r - 3)), layer)
        set_tile(wide_ref, 12 + q, layer)
    set_tile(wide_ref, 15, over + jnp.where(lane < 32, 0.0, turn(far_over, 32)))
    set_tile(wide_ref, 16, jnp.where(lane < 96, 0.0, far_over))


def front_kernel(
    start_hbm, search_hbm, held_ref, ids_ref, kmat_ref, ritz_ref, moduli_ref,
    gram_ref, s_out, r_out, p_out,
    start_in, search_in, stencil_ref, s, r, p, image_s, columns, image, wide, blocks,
    s_pack, p_pack, r_pack, s_came, p_came, r_came,
    s_layer, r_layer, p_layer, s_edge, r_edge, p_edge,
    s_ahead, r_ahead, p_ahead, s_side, r_side, p_side, s_corner, r_corner, p_corner,
    back, back_over, back_corner, back_came, over_came, corner_came,
    whole, g, from_core, half, from_x, quarter, from_y, from_z,
    local, send, recv,
):
    axial, hoop = lax.axis_index("axial"), lax.axis_index("hoop")
    z, x = axial // 4, axial % 4
    y, core = hoop // 2, hoop % 2
    top, bottom = z == 3, z == 0
    lane = lanes_of(K)

    def at(z, x, y, core):
        return (z * 4 + x, y * 2 + core)

    def around(dz, ds):
        sector = (hoop * 4 + x + ds + 32) % 32
        return ((z + dz + 4) % 4 * 4 + sector % 4, sector // 4)

    peers = {
        "core": [at(z, x, y, 1 - core)],
        "x": [at(z, (x + d) % 4, y, core) for d in (1, 2, 3)],
        "y": [at(z, x, (y + d) % 4, core) for d in (1, 2, 3)],
        "z": [at((z + d) % 4, x, y, core) for d in (1, 2, 3)],
        "hoop": [around(0, 1), around(0, -1), around(1, 1), around(-1, -1)],
    }
    loads = [
        pltpu.make_async_copy(start_hbm, start_in, local.at[0]),
        pltpu.make_async_copy(search_hbm, search_in, local.at[1]),
    ]
    for load in loads:
        load.start()
    barrier = pltpu.get_barrier_semaphore()
    count = 0
    for group in peers.values():
        for peer in group:
            pl.semaphore_signal(barrier, inc=1, device_id=peer, device_id_type=MESH)
            count += 1
    used = [0]

    def copy(source, target, peer):
        index = used[0]
        used[0] += 1
        made = pltpu.make_async_remote_copy(
            src_ref=source, dst_ref=target, send_sem=send.at[index], recv_sem=recv.at[index],
            device_id=peer, device_id_type=MESH,
        )
        made.start()
        return made

    def finish(copies):
        for made in copies:
            made.wait()

    def exchange(pack_ref, came_ref):
        copies = []
        for d in (1, 2, 3):
            copies.append(copy(pack_ref.at[(x + d) % 4], came_ref.at[x], peers["x"][d - 1]))
        return copies

    def forward(layer, edge, ahead, side, corner):
        return [
            copy(layer, ahead, around(-1, 0)),
            copy(edge, side, around(0, -1)),
            copy(edge, corner, around(-1, -1)),
        ]

    ids = ids_ref[...]
    coef = jnp.zeros(ids.shape, F32)
    for material in range(3):
        coef = coef + jnp.where(ids == material, moduli_ref[material], 0.0)
    free = (1 - held_ref[...]).astype(F32)
    row = lax.broadcasted_iota(jnp.int32, (8, 128), 0)
    notes = []
    for node in range(4):
        note = jnp.where(row == 0, free[node : node + 1], 0.0)
        notes.append(jnp.where(row == 1, coef[node : node + 1], note) if node < 3 else note)
    for to, value in enumerate(swap(notes)):
        s_pack[to, 288:296, :] = value

    def mask_in(source, field_out):
        for i in range(12):
            set_tile(field_out, i, source[pl.ds(i, K, stride=12), :] * free[i % 4 : i % 4 + 1])

    loads[0].wait()
    mask_in(start_in, s_out)
    pack(s_out, s_pack)
    pl.semaphore_wait(barrier, count)
    flying = exchange(s_pack, s_came)
    s_came[x] = s_pack[x]
    stencil_ref[...] = stencil(kmat_ref[...])
    zero = jnp.zeros((K, 128), F32)
    for high in range(8):
        for low in (6, 7):
            columns[pl.ds(8 * high + low, K, stride=64), :] = zero
    loads[1].wait()
    mask_in(search_in, p_out)
    pack(p_out, p_pack)
    finish(flying)

    unpack(s_came, s)
    notes = swap([s_came[j, 288:296, :] for j in range(4)])
    free = [note[0:1] for note in notes]
    coef = jnp.concatenate([note[1:2] for note in notes[:3]], 0)
    first_nodes(s, s_layer, s_edge)
    flying = forward(s_layer, s_edge, s_ahead, s_side, s_corner)
    p_flying = exchange(p_pack, p_came)
    p_came[x] = p_pack[x]

    def keep(index, value):
        blocks[index, :, 0:K] = value

    keep(0, mm_nt(s[...], s[...]))
    finish(flying)
    corner, far_edge = far_edges(s_side[...], s_corner[...], top)
    put(columns, s, s_ahead, s_side[...], far_edge, top)
    products(columns, image, stencil_ref, coef)
    take(image, wide)
    for q in range(3):
        back[96 * q : 96 * q + 96, :] = tile(wide, 12 + q)
    back_over[...] = tile(wide, 15)
    back_corner[...] = tile(wide, 16)
    flying = [
        copy(back, back_came, around(1, 0)),
        copy(back_over, over_came, around(0, 1)),
        copy(back_corner, corner_came, around(1, 1)),
    ]

    finish(p_flying)
    unpack(p_came, p)
    first_nodes(p, p_layer, p_edge)
    p_flying = forward(p_layer, p_edge, p_ahead, p_side, p_corner)
    keep(2, mm_nt(s[...], p[...]))
    keep(5, mm_nt(p[...], p[...]))
    finish(flying)

    over = over_came[...] + jnp.where(bottom, 0.0, jnp.where(lane < 32, turn(corner_came[...], 32), 0.0))
    for q in range(3):
        below = jnp.where(bottom, 0.0, back_came[96 * q : 96 * q + 96, :])
        for node in range(4):
            i = 4 * q + node
            value = tile(wide, i) + jnp.where(lane < 32, turn(below, -32 * node), 0.0)
            value = (value + jnp.where(lane % 32 == 0, turn(over, -i), 0.0)) * free[node]
            set_tile(image_s, i, value)
            set_tile(r, i, value - ritz_ref[...] * tile(s, i))
    first_nodes(r, r_layer, r_edge)
    flying = forward(r_layer, r_edge, r_ahead, r_side, r_corner)
    pack(r, r_pack)
    r_flying = exchange(r_pack, r_came)
    r_came[x] = r_pack[x]

    def ext(field, ahead, side, corner):
        layers = [jnp.where(top, 0.0, ahead[96 * q : 96 * q + 96, :]) for q in range(3)]
        return jnp.concatenate([field[...]] + layers + [side[...], corner], 1)

    finish(p_flying)
    corner, far_edge = far_edges(p_side[...], p_corner[...], top)
    put(columns, p, p_ahead, p_side[...], far_edge, top)
    products(columns, image, stencil_ref, coef)
    take(image, wide)
    p_ext = ext(p, p_ahead, p_side, corner)
    keep(11, mm_nt(wide[...], p_ext))
    for index, left, right in ((6, image_s, s), (7, image_s, r), (8, image_s, p), (1, s, r), (3, r, r), (4, r, p)):
        keep(index, mm_nt(left[...], right[...]))
    finish(flying)
    corner, far_edge = far_edges(r_side[...], r_corner[...], top)
    put(columns, r, r_ahead, r_side[...], far_edge, top)
    products(columns, image, stencil_ref, coef)
    take(image, wide)
    keep(9, mm_nt(wide[...], ext(r, r_ahead, r_side, corner)))
    keep(10, mm_nt(wide[...], ext(p, p_ahead, p_side, far_edges(p_side[...], p_corner[...], top)[0])))

    for group in range(3):
        extra = jnp.where(lane < K, blocks[9 + group], 0.0)
        for j in range(3):
            both = jnp.where(lane < K, blocks[3 * group + j], turn(extra, 96 - 32 * j))
            first = 12 * (3 * group + j)
            g[first : first + 12] = both.reshape(12, 8, 128)
    g[108:128] = jnp.zeros((20, 8, 128), F32)

    finish([copy(g.at[pl.ds((1 - core) * 64, 64)], from_core, peers["core"][0])])
    half[...] = g[pl.ds(core * 64, 64)] + from_core[...]
    finish([copy(half.at[pl.ds((x + d) % 4 * 16, 16)], from_x.at[d - 1], peers["x"][d - 1]) for d in (1, 2, 3)])
    quarter[...] = (half[pl.ds(x * 16, 16)] + from_x[0]) + (from_x[1] + from_x[2])
    finish([copy(quarter.at[pl.ds((y + d) % 4 * 4, 4)], from_y.at[d - 1], peers["y"][d - 1]) for d in (1, 2, 3)])
    from_z[z] = (quarter[pl.ds(y * 4, 4)] + from_y[0]) + (from_y[1] + from_y[2])
    finish([copy(from_z.at[z], from_z.at[z], peer) for peer in peers["z"]])
    base = core * 64 + x * 16 + y * 4
    whole[pl.ds(base, 4)] = (from_z[0] + from_z[1]) + (from_z[2] + from_z[3])
    for axis, first, size in (("y", base, 4), ("x", core * 64 + x * 16, 16), ("core", core * 64, 64)):
        part = whole.at[pl.ds(first, size)]
        finish([copy(part, part, peer) for peer in peers[axis]])
    gram_ref[...] = whole[...]
    finish(r_flying)
    unpack(r_came, r_out)


def front(start, search, held, ids, kmat, ritz, moduli):
    def rows(*shape):
        return pltpu.VMEM(shape + (128,), F32)

    field = pltpu.VMEM((K, 1536), F32)
    anywhere = pl.BlockSpec(memory_space=pl.ANY)
    return pl.pallas_call(
        front_kernel,
        out_shape=[jax.ShapeDtypeStruct((128, 8, 128), F32)] + [jax.ShapeDtypeStruct((K, 1536), F32)] * 3,
        in_specs=[anywhere] * 2 + [VMEM] * 4 + [SMEM],
        out_specs=[VMEM] * 4,
        scratch_shapes=[rows(1152)] * 2
        + [pltpu.VMEM((96, 384), BF16)]
        + [field] * 4
        + [rows(K * 64)] * 2
        + [pltpu.VMEM((K, 17 * 128), F32), rows(12, K)]
        + [rows(4, 296), rows(4, 288), rows(4, 288)] * 2
        + [rows(288)] * 3 + [rows(K)] * 3
        + [rows(288)] * 3 + [rows(K)] * 6
        + [rows(288), rows(K), rows(K)] * 2
        + [rows(n, 8) for n in (128, 128, 64, 64)]
        + [rows(3, 16, 8), rows(16, 8), rows(3, 4, 8), rows(4, 4, 8)]
        + [pltpu.SemaphoreType.DMA((2,)), pltpu.SemaphoreType.DMA((COPIES,)), pltpu.SemaphoreType.DMA((COPIES,))],
        compiler_params=pltpu.CompilerParams(vmem_limit_bytes=ROOM, collective_id=0, has_side_effects=True),
        name="front",
    )(start, search, held, ids, kmat, ritz, moduli)


def unpack_gram(gram_ref):
    lane = lanes_of(K)
    blocks = [None] * 12
    for group in range(3):
        extra = jnp.zeros((K, 128), F32)
        for j in range(3):
            first = 12 * (3 * group + j)
            both = gram_ref[first : first + 12].reshape(K, 128)
            blocks[3 * group + j] = jnp.where(lane < K, both, 0.0)
            here = (lane >= 32 * j) & (lane < 32 * j + 32)
            extra = jnp.where(here, turn(both, 32 + 32 * j), extra)
        blocks[9 + group] = extra
    return blocks


def dense_kernel(gram_ref, s_ref, r_ref, p_ref, block_ref, search_ref, rot_ref):
    rotation(unpack_gram(gram_ref), math.sqrt(UNKNOWNS), rot_ref)
    rot = rot_ref[...]
    for i in range(6):
        lanes = slice(256 * i, 256 * i + 256)
        tail = mm(rot[:, K:], jnp.concatenate([r_ref[:, lanes], p_ref[:, lanes]], 0))
        head = tail + mm(rot[:, :K], s_ref[:, lanes])
        for h in range(2):
            block_ref[pl.ds(2 * i + h, K, stride=12), :] = head[:, 128 * h : 128 * h + 128]
            search_ref[pl.ds(2 * i + h, K, stride=12), :] = tail[:, 128 * h : 128 * h + 128]


def dense(gram, s, r, p):
    return pl.pallas_call(
        dense_kernel,
        out_shape=[jax.ShapeDtypeStruct((1152, 128), F32)] * 2,
        in_specs=[VMEM] * 4,
        out_specs=[VMEM] * 2,
        scratch_shapes=[pltpu.VMEM((K, 288), F32)],
        compiler_params=pltpu.CompilerParams(vmem_limit_bytes=ROOM),
        name="dense",
    )(gram, s, r, p)


def on_device(start_block, search_block, ritz_values, element_matrix, moduli, material_ids, held):
    shape = start_block.shape
    gram, s, r, p = front(
        start_block.reshape(1152, 128), search_block.reshape(1152, 128), held.reshape(4, 128),
        material_ids.reshape(3, 128), element_matrix, ritz_values.reshape(K, 1), moduli,
    )
    block, search = dense(gram, s, r, p)
    return block.reshape(shape), search.reshape(shape)


def solution(mesh):
    split_field = P(None, None, None, "axial", "hoop")
    split_nodes = P(None, "axial", "hoop")
    in_specs = (split_field, split_field, P(), P(), P(), split_nodes, split_nodes)
    return jax.shard_map(
        on_device, mesh=mesh, in_specs=in_specs, out_specs=(split_field, split_field), check_vma=False
    )
```

```python
import functools
import math

import jax
import jax.numpy as jnp
from jax import lax
from jax.experimental import pallas as pl
from jax.experimental.pallas import tpu as pltpu
from jax.sharding import PartitionSpec as P

HI = lax.Precision.HIGHEST
MESH = pl.DeviceIdType.MESH
K = 96
F32 = jnp.float32
BF16 = jnp.bfloat16
VMEM = pl.BlockSpec(memory_space=pltpu.VMEM)
SMEM = pl.BlockSpec(memory_space=pltpu.SMEM)
HBM = pl.BlockSpec(memory_space=pltpu.HBM)
ROOM = 62 * 2**20
UNKNOWNS = 196608
UNROLL = 12
COPIES = 60
PLANE = [(dx, dy) for dx in (2, 1, 3, 0) for dy in (2, 1, 3, 0) if (dx, dy) != (0, 0)]


def sweep(block, factor=True):
    lane = lax.broadcasted_iota(jnp.int32, (8, 128), 1)
    sub = lax.broadcasted_iota(jnp.int32, (8, 128), 0)
    tiles = [block[8 * t : 8 * t + 8, :] for t in range(12)]

    def spread(value, at):
        return [jnp.broadcast_to(value[:, at + j : at + j + 1], (8, 128)) for j in range(4)]

    def pick(column, at):
        return jnp.broadcast_to(column[at : at + 1, :], (8, 128))

    def square(at):
        wide = spread(tiles[at // 8], at)
        return [[pick(wide[j], at % 8 + i) if j >= i else None for j in range(4)] for i in range(4)]

    found = []
    pivot = square(0)
    for group in range(24):
        p = 4 * group
        home, low = p // 8, p % 8
        below = range(home if low == 0 else home + 1, 12)
        cols = {t: spread(tiles[t], p) for t in below}
        (a00, a01, b00, b01), (_, a11, b10, b11), (_, _, c00, c01), (_, _, _, c11) = pivot
        ia = pl.reciprocal(a00 * a11 - a01 * a01)
        h00, h01, h11 = a11 * ia, -a01 * ia, a00 * ia
        x00, x01 = h00 * b00 + h01 * b10, h00 * b01 + h01 * b11
        x10, x11 = h01 * b00 + h11 * b10, h01 * b01 + h11 * b11
        s00 = c00 - (b00 * x00 + b10 * x10)
        s01 = c01 - (b00 * x01 + b10 * x11)
        s11 = c11 - (b01 * x01 + b11 * x11)
        ic = pl.reciprocal(s00 * s11 - s01 * s01)
        g00, g01, g11 = s11 * ic, -s01 * ic, s00 * ic

        def solve(f0, f1, f2, f3):
            u0 = f2 - (x00 * f0 + x10 * f1)
            u1 = f3 - (x01 * f0 + x11 * f1)
            n2 = g00 * u0 + g01 * u1
            n3 = g01 * u0 + g11 * u1
            n0 = (h00 * f0 + h01 * f1) - (x00 * n2 + x01 * n3)
            n1 = (h01 * f0 + h11 * f1) - (x10 * n2 + x11 * n3)
            return [n0, n1, n2, n3], u0, u1

        if group < 23:
            q = p + 4
            old = square(q)
            ahead = [[pick(cols[q // 8][i], q % 8 + j) for i in range(4)] for j in range(4)]
            factors = [solve(*ahead[j])[0] for j in range(4)]
            pivot = [
                [
                    old[i][j]
                    - ((ahead[i][0] * factors[j][0] + ahead[i][1] * factors[j][1])
                       + (ahead[i][2] * factors[j][2] + ahead[i][3] * factors[j][3]))
                    if j >= i else None
                    for j in range(4)
                ]
                for i in range(4)
            ]
        picked = (lane >= p) & (lane < p + 4)
        full = [jnp.where(picked, jnp.where(lane == p + j, 1.0, 0.0), pick(tiles[home], low + j)) for j in range(4)]
        new, u0, u1 = solve(*full)
        left = [jnp.where(lane < p + 4, f, 0.0) for f in full[:2]]
        y0, y1 = (jnp.where(lane < p + 4, u, 0.0) for u in (u0, u1))
        ra, rs = pl.reciprocal(a00), pl.reciprocal(s00)
        e1, e3 = a11 - a01 * a01 * ra, s11 - s01 * s01 * rs
        found.append(
            [
                left[0] * lax.rsqrt(a00),
                (left[1] - a01 * ra * left[0]) * lax.rsqrt(e1),
                y0 * lax.rsqrt(s00),
                (y1 - s01 * rs * y0) * lax.rsqrt(e3),
            ]
        )
        for t in below:
            c = cols[t]
            tiles[t] = jnp.where(picked, 0.0, tiles[t]) - (
                (c[0] * new[0] + c[1] * new[1]) + (c[2] * new[2] + c[3] * new[3])
            )
    out = []
    for t in range(12):
        eight = found[2 * t] + found[2 * t + 1]
        whole = eight[0]
        for s in range(1, 8):
            whole = jnp.where(sub == s, eight[s], whole)
        out.append(whole)
    return jnp.concatenate(out, 0)


def mm(a, b):
    return lax.dot_general(a, b, (((1,), (0,)), ((), ())), precision=HI, preferred_element_type=F32)


def diagonal(block):
    lane = lax.broadcasted_iota(jnp.int32, (K, 128), 1)
    row = lax.broadcasted_iota(jnp.int32, (K, 128), 0)
    only = jnp.where(lane == row, block, 0.0)
    down = jnp.sum(only, 1, keepdims=True)
    along = jnp.sum(only, 0, keepdims=True)
    return lax.rsqrt(down), lax.rsqrt(jnp.where(along == 0.0, 1.0, along))


def cut(block):
    return block[:, :K]


def pad(block):
    return jnp.concatenate([block, jnp.zeros((block.shape[0], 128 - block.shape[1]), F32)], 1)


def rotation(b, a, scale, rot_ref):
    m = [x + y for x, y in zip(a, b)]
    d1, e1 = diagonal(m[0])
    d2, e2 = diagonal(m[3])
    d3, e3 = diagonal(m[5])
    b21, b31, b32 = (pad(cut(x).T) for x in (b[1], b[2], b[4]))
    f1, f2, f3 = b[0] * d1, b21 * d2, b31 * d3
    v1 = cut(sweep(m[0] * d1 * e1))
    z1 = mm(v1, jnp.concatenate([m[1] * d1 * e2, m[2] * d1 * e3, f1], 1))
    z12, z13, y1 = cut(z1), cut(z1[:, 128:]), z1[:, 256:]
    s2 = jnp.concatenate([m[3] * d2 * e2, m[4] * d2 * e3, f2], 1) - mm(z12.T, z1)
    s3 = jnp.concatenate([m[5] * d3 * e3, f3], 1) - mm(z13.T, z1[:, 128:])
    v2 = cut(sweep(s2[:, :128]))
    z2 = mm(v2, s2[:, 128:])
    z23, y2 = cut(z2), z2[:, 128:]
    s3 = s3 - mm(z23.T, z2)
    v3 = cut(sweep(s3[:, :128]))
    w3 = mm(v3.T, mm(v3, s3[:, 128:]))
    w2 = mm(v2.T, y2 - mm(z23, w3))
    w1 = mm(v1.T, y1 - mm(jnp.concatenate([z12, z13], 1), jnp.concatenate([w2, w3], 0)))
    w = jnp.concatenate([w1 * d1, w2 * d2, w3 * d3], 0)
    big = jnp.concatenate(
        [
            jnp.concatenate([cut(b[0]), cut(b[1]), cut(b[2])], 1),
            jnp.concatenate([cut(b21), cut(b[3]), cut(b[4])], 1),
            jnp.concatenate([cut(b31), cut(b32), cut(b[5])], 1),
        ],
        0,
    )
    wt = cut(w).T
    small = mm(wt, mm(big, w))
    ds, es = diagonal(small)
    inv = sweep(small * ds * es) * es
    rot_ref[...] = mm(cut(inv), wt) * scale


def mm_nt(a, b):
    return lax.dot_general(a, b, (((1,), (1,)), ((), ())), precision=HI, preferred_element_type=F32)


def split(x):
    high = x.astype(BF16)
    rest = x - high.astype(F32)
    middle = rest.astype(BF16)
    low = (rest - middle.astype(F32)).astype(BF16)
    return high, middle, low


def stencil(kmat):
    def rows_of(shape, axis):
        at = lax.broadcasted_iota(jnp.int32, shape, axis)
        low, high = at % 8, at // 8
        dh, high = high % 2, high // 2
        return low // 3, low % 3, dh, high % 3, high // 3, low < 6

    def columns_of(shape, axis):
        at = lax.broadcasted_iota(jnp.int32, shape, axis)
        low, high = at % 8, at // 8
        return low // 3, low % 3, high // 4, high % 4, low < 6

    da, q, dh, _, dr, real = rows_of((96, 24), 0)
    corner = lax.broadcasted_iota(jnp.int32, (96, 24), 1)
    pick = jnp.where(real & (corner == 3 * (4 * dr + 2 * da + dh) + q), 1.0, 0.0)
    picked = mm(pick, kmat)
    layer = rows_of((96, 64), 0)[3]
    node = columns_of((96, 64), 1)[3]
    total = jnp.zeros((96, 64), F32)
    for dr in range(2):
        da, q, dh, _, real = columns_of((24, 64), 1)
        corner = lax.broadcasted_iota(jnp.int32, (24, 64), 0)
        place = jnp.where(real & (corner == 3 * (4 * dr + 2 * da + dh) + q), 1.0, 0.0)
        total = total + jnp.where(node == layer + dr, mm(picked, place), 0.0)
    high, middle, low = split(total)
    return jnp.concatenate([high, high, high, middle, middle, low], 1)


def lanes_of(rows):
    return lax.broadcasted_iota(jnp.int32, (rows, 128), 1)


def turn(x, by):
    return pltpu.roll(x, by % 128, 1) if by % 128 else x


def swap(tiles):
    lane = lanes_of(tiles[0].shape[0])
    front, even = lane < 64, (lane // 32) % 2 == 0
    a, b, c, d = tiles
    a, c = jnp.where(front, a, turn(c, 64)), jnp.where(front, turn(a, 64), c)
    b, d = jnp.where(front, b, turn(d, 64)), jnp.where(front, turn(b, 64), d)
    a, b = jnp.where(even, a, turn(b, 32)), jnp.where(even, turn(a, 96), b)
    c, d = jnp.where(even, c, turn(d, 32)), jnp.where(even, turn(c, 96), d)
    return a, b, c, d


def tile(ref, i):
    return ref[:, 128 * i : 128 * i + 128]


def set_tile(ref, i, value):
    ref[:, 128 * i : 128 * i + 128] = value


def pack(field_ref, pack_ref):
    for q in range(3):
        for to, value in enumerate(swap([tile(field_ref, 4 * q + r) for r in range(4)])):
            pack_ref[to, 96 * q : 96 * q + 96, :] = value


def unpack(came_ref, field_ref):
    for q in range(3):
        for r, value in enumerate(swap([came_ref[j, 96 * q : 96 * q + 96, :] for j in range(4)])):
            set_tile(field_ref, 4 * q + r, value)


def first_nodes(field_ref, layer_ref, edge_ref):
    lane = lanes_of(K)
    edge = jnp.zeros((K, 128), F32)
    for q in range(3):
        layer = jnp.zeros((K, 128), F32)
        for r in range(4):
            value = tile(field_ref, 4 * q + r)
            layer = jnp.where(lane // 32 == r, turn(value, 32 * r), layer)
            edge = jnp.where(lane % 32 == 4 * q + r, turn(value, 4 * q + r), edge)
        layer_ref[96 * q : 96 * q + 96, :] = layer
    edge_ref[...] = edge


def put(columns_ref, field_ref, layer_ref, edge, far_edge, top):
    lane = lanes_of(K)
    for q in range(3):
        for r in range(4):
            i = 4 * q + r
            near = tile(field_ref, i)
            ahead = jnp.where(top, 0.0, turn(layer_ref[96 * q : 96 * q + 96, :], 32 * (3 - r)))
            far = jnp.where(lane < 96, turn(near, 96), ahead)
            for da, (value, side) in enumerate(((near, edge), (far, far_edge))):
                at = 8 * r + 3 * da + q
                columns_ref[pl.ds(at, K, stride=64), :] = value
                moved = jnp.where(lane % 32 == 31, turn(side, 31 - i), turn(value, 127))
                columns_ref[pl.ds(32 + at, K, stride=64), :] = moved


def far_edges(edge, corner, top):
    lane = lanes_of(K)
    corner = jnp.where(top, 0.0, jnp.where(lane < 96, 0.0, turn(corner, 96)))
    return corner, jnp.where(lane < 96, turn(edge, 96), corner)


def products(columns_ref, image_ref, stencil_ref, coef):
    weights = stencil_ref[...]
    coef = [jnp.broadcast_to(coef[r : r + 1], (8, 128)) for r in range(3)]
    wide = 8

    def step(group, carry):
        base = pl.multiple_of(64 * wide * group, 64 * wide)
        some = columns_ref[pl.ds(base, 64 * wide), :]
        high, middle, low = split(jnp.concatenate([some[64 * c : 64 * c + 64] for c in range(wide)], 1))
        stack = jnp.concatenate([high, middle, low, high, middle, high], 0)
        terms = jnp.dot(weights, stack, preferred_element_type=F32)
        for c in range(wide):
            term = terms[:, 128 * c : 128 * c + 128]

            def part(dr, r, dh):
                at = 8 * ((dr * 3 + r) * 2 + dh)
                return term[at : at + 8] * coef[r]

            values = []
            for dh in range(2):
                for node in range(4):
                    parts = [part(dr, node - dr, dh) for dr in range(2) if 0 <= node - dr < 3]
                    values.append(parts[0] if len(parts) == 1 else parts[0] + parts[1])
            image_ref[pl.ds(base + 64 * c, 64), :] = jnp.concatenate(values, 0)
        return carry

    lax.fori_loop(0, K // wide, step, 0, unroll=UNROLL)


def take(image_ref, wide_ref):
    lane = lanes_of(K)
    over, far_over = jnp.zeros((K, 128), F32), jnp.zeros((K, 128), F32)
    for q in range(3):
        layer = jnp.zeros((K, 128), F32)
        for r in range(4):
            i = 4 * q + r
            at = 8 * r + q

            def shifted_sum(at):
                second = image_ref[pl.ds(32 + at, K, stride=64), :]
                first = image_ref[pl.ds(at, K, stride=64), :]
                return first + jnp.where(lane % 32 == 0, 0.0, turn(second, 1)), turn(second, i - 31)

            near, out = shifted_sum(at)
            far, far_out = shifted_sum(at + 3)
            over = jnp.where(lane % 32 == i, out, over)
            far_over = jnp.where(lane % 32 == i, far_out, far_over)
            set_tile(wide_ref, i, near + jnp.where(lane < 32, 0.0, turn(far, 32)))
            layer = jnp.where(lane // 32 == r, turn(far, 32 * (r - 3)), layer)
        set_tile(wide_ref, 12 + q, layer)
    set_tile(wide_ref, 15, over + jnp.where(lane < 32, 0.0, turn(far_over, 32)))
    set_tile(wide_ref, 16, jnp.where(lane < 96, 0.0, far_over))


def front_kernel(
    start_hbm, search_hbm, held_hbm, ids_hbm, kmat_hbm, ritz_hbm, moduli_hbm,
    gram_ref, s_hbm, r_hbm, p_hbm,
    s_out, r_out, p_out,
    start_in, search_in, held_ref, ids_ref, kmat_ref, ritz_row, moduli_ref, ritz_ref, stencil_ref, s, r, p, image_s, columns, image, wide, blocks,
    s_pack, p_pack, r_pack, s_came, p_came, r_came,
    s_layer, r_layer, p_layer, s_edge, r_edge, p_edge,
    s_ahead, r_ahead, p_ahead, s_side, r_side, p_side, s_corner, r_corner, p_corner,
    back, back_over, back_corner, back_came, over_came, corner_came,
    whole, g, from_core, half, from_plane, from_z,
    local, send, recv,
):
    axial, hoop = lax.axis_index("axial"), lax.axis_index("hoop")
    z, x = axial // 4, axial % 4
    y, core = hoop // 2, hoop % 2
    top, bottom = z == 3, z == 0
    lane = lanes_of(K)

    def at(z, x, y, core):
        return (z * 4 + x, y * 2 + core)

    def around(dz, ds):
        sector = (hoop * 4 + x + ds + 32) % 32
        return ((z + dz + 4) % 4 * 4 + sector % 4, sector // 4)

    peers = {
        "core": [at(z, x, y, 1 - core)],
        "plane": [at(z, (x + dx) % 4, (y + dy) % 4, core) for dx, dy in PLANE],
        "z": [at((z + d) % 4, x, y, core) for d in (1, 2, 3)],
        "hoop": [around(0, 1), around(0, -1), around(1, 1), around(-1, -1)],
    }
    pairs = (
        (start_hbm, start_in), (search_hbm, search_in), (held_hbm, held_ref), (ids_hbm, ids_ref),
        (kmat_hbm, kmat_ref), (ritz_hbm, ritz_row), (moduli_hbm, moduli_ref),
    )
    loads = [pltpu.make_async_copy(source, target, local.at[n]) for n, (source, target) in enumerate(pairs)]
    for load in loads:
        load.start()
    barrier = pltpu.get_barrier_semaphore()
    count = 0
    for group in peers.values():
        for peer in group:
            pl.semaphore_signal(barrier, inc=1, device_id=peer, device_id_type=MESH)
            count += 1
    used = [0]

    def copy(source, target, peer):
        index = used[0]
        used[0] += 1
        made = pltpu.make_async_remote_copy(
            src_ref=source, dst_ref=target, send_sem=send.at[index], recv_sem=recv.at[index],
            device_id=peer, device_id_type=MESH,
        )
        made.start()
        return made

    def finish(copies):
        for made in copies:
            made.wait()

    def exchange(pack_ref, came_ref):
        copies = []
        for d in (2, 1, 3):
            copies.append(copy(pack_ref.at[(x + d) % 4], came_ref.at[x], at(z, (x + d) % 4, y, core)))
        return copies

    def forward(layer, edge, ahead, side, corner):
        return [
            copy(layer, ahead, around(-1, 0)),
            copy(edge, side, around(0, -1)),
            copy(edge, corner, around(-1, -1)),
        ]

    for load in loads[2:]:
        load.wait()
    coef = []
    for layer in range(3):
        ids = ids_ref[layer]
        total = jnp.zeros((1, 128), F32)
        for material in range(3):
            total = total + jnp.where(ids == material, moduli_ref[0:1, material : material + 1], 0.0)
        coef.append(total)
    free = [(1 - held_ref[node]).astype(F32) for node in range(4)]
    ritz = jnp.broadcast_to(jnp.concatenate([ritz_row[...], jnp.zeros((1, 32), F32)], 1), (K, 128))
    ritz_ref[...] = jnp.sum(jnp.where(lane == lax.broadcasted_iota(jnp.int32, (K, 128), 0), ritz, 0.0), 1, keepdims=True)
    row = lax.broadcasted_iota(jnp.int32, (8, 128), 0)
    notes = []
    for node in range(4):
        note = jnp.where(row == 0, free[node], 0.0)
        notes.append(jnp.where(row == 1, coef[node], note) if node < 3 else note)
    for to, value in enumerate(swap(notes)):
        s_pack[to, 288:296, :] = value

    def mask_in(source, field_out):
        for i in range(12):
            set_tile(field_out, i, source[pl.ds(i, K, stride=12), :] * free[i % 4])

    loads[0].wait()
    mask_in(start_in, s_out)
    pack(s_out, s_pack)
    pl.semaphore_wait(barrier, count)
    flying = exchange(s_pack, s_came)
    s_came[x] = s_pack[x]
    stencil_ref[...] = stencil(kmat_ref[...])
    zero = jnp.zeros((K, 128), F32)
    for high in range(8):
        for low in (6, 7):
            columns[pl.ds(8 * high + low, K, stride=64), :] = zero
    loads[1].wait()
    mask_in(search_in, p_out)
    pack(p_out, p_pack)
    p_flying = exchange(p_pack, p_came)
    p_came[x] = p_pack[x]
    stores = [
        pltpu.make_async_copy(s_out, s_hbm, local.at[7]),
        pltpu.make_async_copy(p_out, p_hbm, local.at[8]),
    ]
    for store in stores:
        store.start()
    finish(flying)

    unpack(s_came, s)
    notes = swap([s_came[j, 288:296, :] for j in range(4)])
    free = [note[0:1] for note in notes]
    coef = jnp.concatenate([note[1:2] for note in notes[:3]], 0)
    first_nodes(s, s_layer, s_edge)
    flying = forward(s_layer, s_edge, s_ahead, s_side, s_corner)

    def keep(index, value):
        blocks[index, :, 0:K] = value

    keep(0, mm_nt(s[...], s[...]))
    finish(flying)
    corner, far_edge = far_edges(s_side[...], s_corner[...], top)
    put(columns, s, s_ahead, s_side[...], far_edge, top)
    products(columns, image, stencil_ref, coef)
    take(image, wide)
    for q in range(3):
        back[96 * q : 96 * q + 96, :] = tile(wide, 12 + q)
    back_over[...] = tile(wide, 15)
    back_corner[...] = tile(wide, 16)
    flying = [
        copy(back, back_came, around(1, 0)),
        copy(back_over, over_came, around(0, 1)),
        copy(back_corner, corner_came, around(1, 1)),
    ]

    finish(p_flying)
    unpack(p_came, p)
    first_nodes(p, p_layer, p_edge)
    p_flying = forward(p_layer, p_edge, p_ahead, p_side, p_corner)
    keep(1, mm_nt(s[...], p[...]))
    keep(3, mm_nt(p[...], p[...]))
    finish(flying)

    over = over_came[...] + jnp.where(bottom, 0.0, jnp.where(lane < 32, turn(corner_came[...], 32), 0.0))
    for q in range(3):
        below = jnp.where(bottom, 0.0, back_came[96 * q : 96 * q + 96, :])
        for node in range(4):
            i = 4 * q + node
            value = tile(wide, i) + jnp.where(lane < 32, turn(below, -32 * node), 0.0)
            value = (value + jnp.where(lane % 32 == 0, turn(over, -i), 0.0)) * free[node]
            set_tile(image_s, i, value)
            set_tile(r, i, value - ritz_ref[...] * tile(s, i))
    first_nodes(r, r_layer, r_edge)
    flying = forward(r_layer, r_edge, r_ahead, r_side, r_corner)
    pack(r, r_pack)
    r_flying = exchange(r_pack, r_came)
    r_came[x] = r_pack[x]

    def ext(field, ahead, side, corner):
        layers = [jnp.where(top, 0.0, ahead[96 * q : 96 * q + 96, :]) for q in range(3)]
        return jnp.concatenate([field[...]] + layers + [side[...], corner], 1)

    finish(p_flying)
    corner, far_edge = far_edges(p_side[...], p_corner[...], top)
    put(columns, p, p_ahead, p_side[...], far_edge, top)
    products(columns, image, stencil_ref, coef)
    take(image, wide)
    p_ext = ext(p, p_ahead, p_side, corner)
    keep(9, mm_nt(wide[...], p_ext))
    for index, left, right in ((6, image_s, s), (7, image_s, p), (8, image_s, r), (2, s, r), (5, r, r), (4, p, r)):
        keep(index, mm_nt(left[...], right[...]))
    finish(flying)
    corner, far_edge = far_edges(r_side[...], r_corner[...], top)
    put(columns, r, r_ahead, r_side[...], far_edge, top)
    products(columns, image, stencil_ref, coef)
    take(image, wide)
    keep(11, mm_nt(wide[...], ext(r, r_ahead, r_side, corner)))
    p_ext = ext(p, p_ahead, p_side, far_edges(p_side[...], p_corner[...], top)[0])
    keep(10, mm_nt(p_ext, wide[...]))

    for group in range(3):
        extra = jnp.where(lane < K, blocks[9 + group], 0.0)
        for j in range(3):
            both = jnp.where(lane < K, blocks[3 * group + j], turn(extra, 96 - 32 * j))
            first = 12 * (3 * group + j)
            g[first : first + 12] = both.reshape(12, 8, 128)
    g[108:128] = jnp.zeros((20, 8, 128), F32)

    finish([copy(g.at[pl.ds((1 - core) * 64, 64)], from_core, peers["core"][0])])
    half[...] = g[pl.ds(core * 64, 64)] + from_core[...]
    copies = []
    for n, ((dx, dy), peer) in enumerate(zip(PLANE, peers["plane"])):
        part = ((x + dx) % 4 * 4 + (y + dy) % 4) * 4
        copies.append(copy(half.at[pl.ds(part, 4)], from_plane.at[n], peer))
    finish(copies)
    parts = [half[pl.ds((x * 4 + y) * 4, 4)]] + [from_plane[n] for n in range(15)]
    while len(parts) > 1:
        parts = [parts[n] + parts[n + 1] for n in range(0, len(parts), 2)]
    from_z[z] = parts[0]
    finish([copy(from_z.at[z], from_z.at[z], peer) for peer in peers["z"]])
    base = core * 64 + (x * 4 + y) * 4
    whole[pl.ds(base, 4)] = (from_z[0] + from_z[1]) + (from_z[2] + from_z[3])
    for axis, first, size in (("plane", base, 4), ("core", core * 64, 64)):
        part = whole.at[pl.ds(first, size)]
        finish([copy(part, part, peer) for peer in peers[axis]])
    gram_ref[...] = whole[...]
    finish(r_flying)
    unpack(r_came, r_out)
    stores.append(pltpu.make_async_copy(r_out, r_hbm, local.at[9]))
    stores[2].start()
    for store in stores:
        store.wait()


def front(start, search, held, ids, kmat, ritz, moduli):
    def rows(*shape):
        return pltpu.VMEM(shape + (128,), F32)

    field = pltpu.VMEM((K, 1536), F32)
    return pl.pallas_call(
        front_kernel,
        out_shape=[jax.ShapeDtypeStruct((128, 8, 128), F32)] + [jax.ShapeDtypeStruct((K, 1536), F32)] * 3,
        in_specs=[HBM] * 7,
        out_specs=[VMEM] + [HBM] * 3,
        scratch_shapes=[field] * 3
        + [rows(1152)] * 2
        + [pltpu.VMEM((n, 1, 128), jnp.int32) for n in (4, 3)]
        + [pltpu.VMEM(shape, F32) for shape in ((24, 24), (1, K), (1, 3), (K, 1))]
        + [pltpu.VMEM((96, 384), BF16)]
        + [field] * 4
        + [rows(K * 64)] * 2
        + [pltpu.VMEM((K, 17 * 128), F32), rows(12, K)]
        + [rows(4, 296), rows(4, 288), rows(4, 288)] * 2
        + [rows(288)] * 3 + [rows(K)] * 3
        + [rows(288)] * 3 + [rows(K)] * 6
        + [rows(288), rows(K), rows(K)] * 2
        + [rows(n, 8) for n in (128, 128, 64, 64)]
        + [rows(15, 4, 8), rows(4, 4, 8)]
        + [pltpu.SemaphoreType.DMA((10,)), pltpu.SemaphoreType.DMA((COPIES,)), pltpu.SemaphoreType.DMA((COPIES,))],
        compiler_params=pltpu.CompilerParams(vmem_limit_bytes=ROOM, collective_id=0, has_side_effects=True),
        name="front",
    )(start, search, held, ids, kmat, ritz, moduli)


def unpack_gram(gram_ref):
    lane = lanes_of(K)
    blocks = [None] * 12
    for group in range(3):
        extra = jnp.zeros((K, 128), F32)
        for j in range(3):
            first = 12 * (3 * group + j)
            both = gram_ref[first : first + 12].reshape(K, 128)
            blocks[3 * group + j] = jnp.where(lane < K, both, 0.0)
            here = (lane >= 32 * j) & (lane < 32 * j + 32)
            extra = jnp.where(here, turn(both, 32 + 32 * j), extra)
        blocks[9 + group] = extra
    return blocks


def dense_kernel(gram_ref, s_hbm, r_hbm, p_hbm, block_ref, search_ref, rot_ref, s_ref, r_ref, p_ref, local):
    loads = [
        pltpu.make_async_copy(source, target, local.at[n])
        for n, (source, target) in enumerate(((s_hbm, s_ref), (r_hbm, r_ref), (p_hbm, p_ref)))
    ]
    for load in loads:
        load.start()
    blocks = unpack_gram(gram_ref)
    rotation(blocks[:6], blocks[6:], math.sqrt(UNKNOWNS), rot_ref)
    rot = rot_ref[...]
    for load in loads:
        load.wait()
    for i in range(6):
        lanes = slice(256 * i, 256 * i + 256)
        tail = mm(rot[:, K:], jnp.concatenate([p_ref[:, lanes], r_ref[:, lanes]], 0))
        head = tail + mm(rot[:, :K], s_ref[:, lanes])
        for h in range(2):
            block_ref[pl.ds(2 * i + h, K, stride=12), :] = head[:, 128 * h : 128 * h + 128]
            search_ref[pl.ds(2 * i + h, K, stride=12), :] = tail[:, 128 * h : 128 * h + 128]


def dense(gram, s, r, p):
    return pl.pallas_call(
        dense_kernel,
        out_shape=[jax.ShapeDtypeStruct((1152, 128), F32)] * 2,
        in_specs=[VMEM] + [HBM] * 3,
        out_specs=[VMEM] * 2,
        scratch_shapes=[pltpu.VMEM((K, 288), F32)] + [pltpu.VMEM((K, 1536), F32)] * 3 + [pltpu.SemaphoreType.DMA((3,))],
        compiler_params=pltpu.CompilerParams(vmem_limit_bytes=ROOM),
        name="dense",
    )(gram, s, r, p)


def on_device(start_block, search_block, ritz_values, element_matrix, moduli, material_ids, held):
    shape = start_block.shape
    gram, s, r, p = front(
        start_block.reshape(1152, 128), search_block.reshape(1152, 128), held,
        material_ids, element_matrix, ritz_values.reshape(1, K), moduli.reshape(1, 3),
    )
    block, search = dense(gram, s, r, p)
    return block.reshape(shape), search.reshape(shape)


def solution(mesh):
    split_field = P(None, None, None, "axial", "hoop")
    split_nodes = P(None, "axial", "hoop")
    in_specs = (split_field, split_field, P(), P(), P(), split_nodes, split_nodes)
    return jax.shard_map(
        on_device, mesh=mesh, in_specs=in_specs, out_specs=(split_field, split_field), check_vma=False
    )
```

```python
import functools
import math

import jax
import jax.numpy as jnp
from jax import lax
from jax.experimental import pallas as pl
from jax.experimental.pallas import tpu as pltpu
from jax.sharding import PartitionSpec as P

HI = lax.Precision.HIGHEST
MESH = pl.DeviceIdType.MESH
K = 96
F32 = jnp.float32
BF16 = jnp.bfloat16
VMEM = pl.BlockSpec(memory_space=pltpu.VMEM)
SMEM = pl.BlockSpec(memory_space=pltpu.SMEM)
HBM = pl.BlockSpec(memory_space=pltpu.HBM)
ROOM = 62 * 2**20
UNKNOWNS = 196608
UNROLL = 12
COPIES = 96
PLANE = [(dx, dy) for dx in (2, 1, 3, 0) for dy in (2, 1, 3, 0) if (dx, dy) != (0, 0)]


def sweep(block, factor=True):
    lane = lax.broadcasted_iota(jnp.int32, (8, 128), 1)
    sub = lax.broadcasted_iota(jnp.int32, (8, 128), 0)
    tiles = [block[8 * t : 8 * t + 8, :] for t in range(12)]

    def spread(value, at):
        return [jnp.broadcast_to(value[:, at + j : at + j + 1], (8, 128)) for j in range(4)]

    def pick(column, at):
        return jnp.broadcast_to(column[at : at + 1, :], (8, 128))

    def square(at):
        wide = spread(tiles[at // 8], at)
        return [[pick(wide[j], at % 8 + i) if j >= i else None for j in range(4)] for i in range(4)]

    found = []
    pivot = square(0)
    for group in range(24):
        p = 4 * group
        home, low = p // 8, p % 8
        below = range(home if low == 0 else home + 1, 12)
        cols = {t: spread(tiles[t], p) for t in below}
        (a00, a01, b00, b01), (_, a11, b10, b11), (_, _, c00, c01), (_, _, _, c11) = pivot
        ia = pl.reciprocal(a00 * a11 - a01 * a01)
        h00, h01, h11 = a11 * ia, -a01 * ia, a00 * ia
        x00, x01 = h00 * b00 + h01 * b10, h00 * b01 + h01 * b11
        x10, x11 = h01 * b00 + h11 * b10, h01 * b01 + h11 * b11
        s00 = c00 - (b00 * x00 + b10 * x10)
        s01 = c01 - (b00 * x01 + b10 * x11)
        s11 = c11 - (b01 * x01 + b11 * x11)
        ic = pl.reciprocal(s00 * s11 - s01 * s01)
        g00, g01, g11 = s11 * ic, -s01 * ic, s00 * ic

        def solve(f0, f1, f2, f3):
            u0 = f2 - (x00 * f0 + x10 * f1)
            u1 = f3 - (x01 * f0 + x11 * f1)
            n2 = g00 * u0 + g01 * u1
            n3 = g01 * u0 + g11 * u1
            n0 = (h00 * f0 + h01 * f1) - (x00 * n2 + x01 * n3)
            n1 = (h01 * f0 + h11 * f1) - (x10 * n2 + x11 * n3)
            return [n0, n1, n2, n3], u0, u1

        if group < 23:
            q = p + 4
            old = square(q)
            ahead = [[pick(cols[q // 8][i], q % 8 + j) for i in range(4)] for j in range(4)]
            factors = [solve(*ahead[j])[0] for j in range(4)]
            pivot = [
                [
                    old[i][j]
                    - ((ahead[i][0] * factors[j][0] + ahead[i][1] * factors[j][1])
                       + (ahead[i][2] * factors[j][2] + ahead[i][3] * factors[j][3]))
                    if j >= i else None
                    for j in range(4)
                ]
                for i in range(4)
            ]
        picked = (lane >= p) & (lane < p + 4)
        full = [jnp.where(picked, jnp.where(lane == p + j, 1.0, 0.0), pick(tiles[home], low + j)) for j in range(4)]
        new, u0, u1 = solve(*full)
        left = [jnp.where(lane < p + 4, f, 0.0) for f in full[:2]]
        y0, y1 = (jnp.where(lane < p + 4, u, 0.0) for u in (u0, u1))
        ra, rs = pl.reciprocal(a00), pl.reciprocal(s00)
        e1, e3 = a11 - a01 * a01 * ra, s11 - s01 * s01 * rs
        found.append(
            [
                left[0] * lax.rsqrt(a00),
                (left[1] - a01 * ra * left[0]) * lax.rsqrt(e1),
                y0 * lax.rsqrt(s00),
                (y1 - s01 * rs * y0) * lax.rsqrt(e3),
            ]
        )
        for t in below:
            c = cols[t]
            tiles[t] = jnp.where(picked, 0.0, tiles[t]) - (
                (c[0] * new[0] + c[1] * new[1]) + (c[2] * new[2] + c[3] * new[3])
            )
    out = []
    for t in range(12):
        eight = found[2 * t] + found[2 * t + 1]
        whole = eight[0]
        for s in range(1, 8):
            whole = jnp.where(sub == s, eight[s], whole)
        out.append(whole)
    return jnp.concatenate(out, 0)


def mm(a, b):
    return lax.dot_general(a, b, (((1,), (0,)), ((), ())), precision=HI, preferred_element_type=F32)


def diagonal(block):
    lane = lax.broadcasted_iota(jnp.int32, (K, 128), 1)
    row = lax.broadcasted_iota(jnp.int32, (K, 128), 0)
    only = jnp.where(lane == row, block, 0.0)
    down = jnp.sum(only, 1, keepdims=True)
    along = jnp.sum(only, 0, keepdims=True)
    return lax.rsqrt(down), lax.rsqrt(jnp.where(along == 0.0, 1.0, along))


def cut(block):
    return block[:, :K]


def pad(block):
    return jnp.concatenate([block, jnp.zeros((block.shape[0], 128 - block.shape[1]), F32)], 1)


def mm_nt(a, b):
    return lax.dot_general(a, b, (((1,), (1,)), ((), ())), precision=HI, preferred_element_type=F32)


def split(x):
    high = x.astype(BF16)
    rest = x - high.astype(F32)
    middle = rest.astype(BF16)
    low = (rest - middle.astype(F32)).astype(BF16)
    return high, middle, low


def stencil(kmat):
    def rows_of(shape, axis):
        at = lax.broadcasted_iota(jnp.int32, shape, axis)
        low, high = at % 8, at // 8
        dh, high = high % 2, high // 2
        return low // 3, low % 3, dh, high % 3, high // 3, low < 6

    def columns_of(shape, axis):
        at = lax.broadcasted_iota(jnp.int32, shape, axis)
        low, high = at % 8, at // 8
        return low // 3, low % 3, high // 4, high % 4, low < 6

    da, q, dh, _, dr, real = rows_of((96, 24), 0)
    corner = lax.broadcasted_iota(jnp.int32, (96, 24), 1)
    pick = jnp.where(real & (corner == 3 * (4 * dr + 2 * da + dh) + q), 1.0, 0.0)
    picked = mm(pick, kmat)
    layer = rows_of((96, 64), 0)[3]
    node = columns_of((96, 64), 1)[3]
    total = jnp.zeros((96, 64), F32)
    for dr in range(2):
        da, q, dh, _, real = columns_of((24, 64), 1)
        corner = lax.broadcasted_iota(jnp.int32, (24, 64), 0)
        place = jnp.where(real & (corner == 3 * (4 * dr + 2 * da + dh) + q), 1.0, 0.0)
        total = total + jnp.where(node == layer + dr, mm(picked, place), 0.0)
    high, middle, low = split(total)
    return jnp.concatenate([high, high, high, middle, middle, low], 1)


def lanes_of(rows):
    return lax.broadcasted_iota(jnp.int32, (rows, 128), 1)


def turn(x, by):
    return pltpu.roll(x, by % 128, 1) if by % 128 else x


def swap(tiles):
    lane = lanes_of(tiles[0].shape[0])
    front, even = lane < 64, (lane // 32) % 2 == 0
    a, b, c, d = tiles
    a, c = jnp.where(front, a, turn(c, 64)), jnp.where(front, turn(a, 64), c)
    b, d = jnp.where(front, b, turn(d, 64)), jnp.where(front, turn(b, 64), d)
    a, b = jnp.where(even, a, turn(b, 32)), jnp.where(even, turn(a, 96), b)
    c, d = jnp.where(even, c, turn(d, 32)), jnp.where(even, turn(c, 96), d)
    return a, b, c, d


def tile(ref, i):
    return ref[:, 128 * i : 128 * i + 128]


def set_tile(ref, i, value):
    ref[:, 128 * i : 128 * i + 128] = value


def pack(field_ref, pack_ref):
    for q in range(3):
        for to, value in enumerate(swap([tile(field_ref, 4 * q + r) for r in range(4)])):
            pack_ref[to, 96 * q : 96 * q + 96, :] = value


def unpack(came_ref, field_ref):
    for q in range(3):
        for r, value in enumerate(swap([came_ref[j, 96 * q : 96 * q + 96, :] for j in range(4)])):
            set_tile(field_ref, 4 * q + r, value)


def first_nodes(field_ref, layer_ref, edge_ref):
    lane = lanes_of(K)
    edge = jnp.zeros((K, 128), F32)
    for q in range(3):
        layer = jnp.zeros((K, 128), F32)
        for r in range(4):
            value = tile(field_ref, 4 * q + r)
            layer = jnp.where(lane // 32 == r, turn(value, 32 * r), layer)
            edge = jnp.where(lane % 32 == 4 * q + r, turn(value, 4 * q + r), edge)
        layer_ref[96 * q : 96 * q + 96, :] = layer
    edge_ref[...] = edge


def put(columns_ref, field_ref, layer_ref, edge, far_edge, top):
    lane = lanes_of(K)
    for q in range(3):
        for r in range(4):
            i = 4 * q + r
            near = tile(field_ref, i)
            ahead = jnp.where(top, 0.0, turn(layer_ref[96 * q : 96 * q + 96, :], 32 * (3 - r)))
            far = jnp.where(lane < 96, turn(near, 96), ahead)
            for da, (value, side) in enumerate(((near, edge), (far, far_edge))):
                at = 8 * r + 3 * da + q
                columns_ref[pl.ds(at, K, stride=64), :] = value
                moved = jnp.where(lane % 32 == 31, turn(side, 31 - i), turn(value, 127))
                columns_ref[pl.ds(32 + at, K, stride=64), :] = moved


def far_edges(edge, corner, top):
    lane = lanes_of(K)
    corner = jnp.where(top, 0.0, jnp.where(lane < 96, 0.0, turn(corner, 96)))
    return corner, jnp.where(lane < 96, turn(edge, 96), corner)


def products(columns_ref, image_ref, stencil_ref, coef):
    weights = stencil_ref[...]
    coef = [jnp.broadcast_to(coef[r : r + 1], (8, 128)) for r in range(3)]
    wide = 8

    def step(group, carry):
        base = pl.multiple_of(64 * wide * group, 64 * wide)
        some = columns_ref[pl.ds(base, 64 * wide), :]
        high, middle, low = split(jnp.concatenate([some[64 * c : 64 * c + 64] for c in range(wide)], 1))
        stack = jnp.concatenate([high, middle, low, high, middle, high], 0)
        terms = jnp.dot(weights, stack, preferred_element_type=F32)
        for c in range(wide):
            term = terms[:, 128 * c : 128 * c + 128]

            def part(dr, r, dh):
                at = 8 * ((dr * 3 + r) * 2 + dh)
                return term[at : at + 8] * coef[r]

            values = []
            for dh in range(2):
                for node in range(4):
                    parts = [part(dr, node - dr, dh) for dr in range(2) if 0 <= node - dr < 3]
                    values.append(parts[0] if len(parts) == 1 else parts[0] + parts[1])
            image_ref[pl.ds(base + 64 * c, 64), :] = jnp.concatenate(values, 0)
        return carry

    lax.fori_loop(0, K // wide, step, 0, unroll=UNROLL)


def take(image_ref, wide_ref):
    lane = lanes_of(K)
    over, far_over = jnp.zeros((K, 128), F32), jnp.zeros((K, 128), F32)
    for q in range(3):
        layer = jnp.zeros((K, 128), F32)
        for r in range(4):
            i = 4 * q + r
            at = 8 * r + q

            def shifted_sum(at):
                second = image_ref[pl.ds(32 + at, K, stride=64), :]
                first = image_ref[pl.ds(at, K, stride=64), :]
                return first + jnp.where(lane % 32 == 0, 0.0, turn(second, 1)), turn(second, i - 31)

            near, out = shifted_sum(at)
            far, far_out = shifted_sum(at + 3)
            over = jnp.where(lane % 32 == i, out, over)
            far_over = jnp.where(lane % 32 == i, far_out, far_over)
            set_tile(wide_ref, i, near + jnp.where(lane < 32, 0.0, turn(far, 32)))
            layer = jnp.where(lane // 32 == r, turn(far, 32 * (r - 3)), layer)
        set_tile(wide_ref, 12 + q, layer)
    set_tile(wide_ref, 15, over + jnp.where(lane < 32, 0.0, turn(far_over, 32)))
    set_tile(wide_ref, 16, jnp.where(lane < 96, 0.0, far_over))


def front_kernel(
    start_hbm, search_hbm, held_hbm, ids_hbm, kmat_hbm, ritz_hbm, moduli_hbm,
    rot_ref, s_hbm, r_hbm, p_hbm,
    s_out, r_out, p_out,
    start_in, search_in, held_ref, ids_ref, kmat_ref, ritz_row, moduli_ref, ritz_ref, stencil_ref, s, r, p, image_s, columns, image, wide, wide_s, early, late,
    s_pack, p_pack, r_pack, s_came, p_came, r_came,
    s_layer, r_layer, p_layer, s_edge, r_edge, p_edge,
    s_ahead, r_ahead, p_ahead, s_side, r_side, p_side, s_corner, r_corner, p_corner,
    back, back_over, back_corner, back_came, over_came, corner_came,
    g, from_core, half, from_plane, from_z, whole,
    g_2, from_core_2, half_2, from_plane_2, from_z_2, whole_2,
    local, send, recv,
):
    axial, hoop = lax.axis_index("axial"), lax.axis_index("hoop")
    z, x = axial // 4, axial % 4
    y, core = hoop // 2, hoop % 2
    top, bottom = z == 3, z == 0
    lane = lanes_of(K)

    def at(z, x, y, core):
        return (z * 4 + x, y * 2 + core)

    def around(dz, ds):
        sector = (hoop * 4 + x + ds + 32) % 32
        return ((z + dz + 4) % 4 * 4 + sector % 4, sector // 4)

    peers = {
        "core": [at(z, x, y, 1 - core)],
        "plane": [at(z, (x + dx) % 4, (y + dy) % 4, core) for dx, dy in PLANE],
        "z": [at((z + d) % 4, x, y, core) for d in (1, 2, 3)],
        "hoop": [around(0, 1), around(0, -1), around(1, 1), around(-1, -1)],
    }
    pairs = (
        (start_hbm, start_in), (search_hbm, search_in), (held_hbm, held_ref), (ids_hbm, ids_ref),
        (kmat_hbm, kmat_ref), (ritz_hbm, ritz_row), (moduli_hbm, moduli_ref),
    )
    loads = [pltpu.make_async_copy(source, target, local.at[n]) for n, (source, target) in enumerate(pairs)]
    for load in loads:
        load.start()
    barrier = pltpu.get_barrier_semaphore()
    count = 0
    for group in peers.values():
        for peer in group:
            pl.semaphore_signal(barrier, inc=1, device_id=peer, device_id_type=MESH)
            count += 1
    used = [0]

    def copy(source, target, peer):
        index = used[0]
        used[0] += 1
        made = pltpu.make_async_remote_copy(
            src_ref=source, dst_ref=target, send_sem=send.at[index], recv_sem=recv.at[index],
            device_id=peer, device_id_type=MESH,
        )
        made.start()
        return made

    def finish(copies):
        for made in copies:
            made.wait()

    def exchange(pack_ref, came_ref):
        copies = []
        for d in (2, 1, 3):
            copies.append(copy(pack_ref.at[(x + d) % 4], came_ref.at[x], at(z, (x + d) % 4, y, core)))
        return copies

    def forward(layer, edge, ahead, side, corner):
        return [
            copy(layer, ahead, around(-1, 0)),
            copy(edge, side, around(0, -1)),
            copy(edge, corner, around(-1, -1)),
        ]

    def summed(g, from_core, half, from_plane, from_z, whole):
        copies = [copy(g.at[pl.ds((1 - core) * 32, 32)], from_core, peers["core"][0])]
        yield
        finish(copies)
        half[...] = g[pl.ds(core * 32, 32)] + from_core[...]
        copies = []
        for n, ((dx, dy), peer) in enumerate(zip(PLANE, peers["plane"])):
            part = ((x + dx) % 4 * 4 + (y + dy) % 4) * 2
            copies.append(copy(half.at[pl.ds(part, 2)], from_plane.at[n], peer))
        yield
        finish(copies)
        parts = [half[pl.ds((x * 4 + y) * 2, 2)]] + [from_plane[n] for n in range(15)]
        while len(parts) > 1:
            parts = [parts[n] + parts[n + 1] for n in range(0, len(parts), 2)]
        from_z[z] = parts[0]
        copies = [copy(from_z.at[z], from_z.at[z], peer) for peer in peers["z"]]
        yield
        finish(copies)
        first = core * 32 + (x * 4 + y) * 2
        whole[pl.ds(first, 2)] = (from_z[0] + from_z[1]) + (from_z[2] + from_z[3])
        part = whole.at[pl.ds(first, 2)]
        copies = [copy(part, part, peer) for peer in peers["plane"]]
        yield
        finish(copies)
        part = whole.at[pl.ds(core * 32, 32)]
        copies = [copy(part, part, peers["core"][0])]
        yield
        finish(copies)

    for load in loads[2:]:
        load.wait()
    coef = []
    for layer in range(3):
        ids = ids_ref[layer]
        total = jnp.zeros((1, 128), F32)
        for material in range(3):
            total = total + jnp.where(ids == material, moduli_ref[0:1, material : material + 1], 0.0)
        coef.append(total)
    free = [(1 - held_ref[node]).astype(F32) for node in range(4)]
    ritz = jnp.broadcast_to(jnp.concatenate([ritz_row[...], jnp.zeros((1, 32), F32)], 1), (K, 128))
    ritz_ref[...] = jnp.sum(jnp.where(lane == lax.broadcasted_iota(jnp.int32, (K, 128), 0), ritz, 0.0), 1, keepdims=True)
    row = lax.broadcasted_iota(jnp.int32, (8, 128), 0)
    notes = []
    for node in range(4):
        note = jnp.where(row == 0, free[node], 0.0)
        notes.append(jnp.where(row == 1, coef[node], note) if node < 3 else note)
    for to, value in enumerate(swap(notes)):
        s_pack[to, 288:296, :] = value

    def mask_in(source, field_out):
        for i in range(12):
            set_tile(field_out, i, source[pl.ds(i, K, stride=12), :] * free[i % 4])

    loads[0].wait()
    mask_in(start_in, s_out)
    pack(s_out, s_pack)
    pl.semaphore_wait(barrier, count)
    flying = exchange(s_pack, s_came)
    s_came[x] = s_pack[x]
    stencil_ref[...] = stencil(kmat_ref[...])
    zero = jnp.zeros((K, 128), F32)
    for high in range(8):
        for low in (6, 7):
            columns[pl.ds(8 * high + low, K, stride=64), :] = zero
    loads[1].wait()
    mask_in(search_in, p_out)
    pack(p_out, p_pack)
    p_flying = exchange(p_pack, p_came)
    p_came[x] = p_pack[x]
    stores = [
        pltpu.make_async_copy(s_out, s_hbm, local.at[7]),
        pltpu.make_async_copy(p_out, p_hbm, local.at[8]),
    ]
    for store in stores:
        store.start()
    finish(flying)

    unpack(s_came, s)
    notes = swap([s_came[j, 288:296, :] for j in range(4)])
    free = [note[0:1] for note in notes]
    coef = jnp.concatenate([note[1:2] for note in notes[:3]], 0)
    first_nodes(s, s_layer, s_edge)
    flying = forward(s_layer, s_edge, s_ahead, s_side, s_corner)

    def keep(blocks, index, value):
        blocks[index, :, 0:K] = value

    keep(early, 0, mm_nt(s[...], s[...]))
    finish(p_flying)
    unpack(p_came, p)
    first_nodes(p, p_layer, p_edge)
    p_flying = forward(p_layer, p_edge, p_ahead, p_side, p_corner)
    keep(early, 1, mm_nt(s[...], p[...]))
    keep(early, 2, mm_nt(p[...], p[...]))
    finish(flying)
    corner, far_edge = far_edges(s_side[...], s_corner[...], top)
    put(columns, s, s_ahead, s_side[...], far_edge, top)
    products(columns, image, stencil_ref, coef)
    take(image, wide_s)
    for q in range(3):
        back[96 * q : 96 * q + 96, :] = tile(wide_s, 12 + q)
    back_over[...] = tile(wide_s, 15)
    back_corner[...] = tile(wide_s, 16)
    flying = [
        copy(back, back_came, around(1, 0)),
        copy(back_over, over_came, around(0, 1)),
        copy(back_corner, corner_came, around(1, 1)),
    ]

    def ext(field, ahead, side, corner):
        layers = [jnp.where(top, 0.0, ahead[96 * q : 96 * q + 96, :]) for q in range(3)]
        return jnp.concatenate([field[...]] + layers + [side[...], corner], 1)

    finish(p_flying)
    p_corner_own, far_edge = far_edges(p_side[...], p_corner[...], top)
    put(columns, p, p_ahead, p_side[...], far_edge, top)
    products(columns, image, stencil_ref, coef)
    take(image, wide)
    keep(early, 5, mm_nt(wide[...], ext(p, p_ahead, p_side, p_corner_own)))

    finish(flying)
    over = over_came[...] + jnp.where(bottom, 0.0, jnp.where(lane < 32, turn(corner_came[...], 32), 0.0))
    for q in range(3):
        below = jnp.where(bottom, 0.0, back_came[96 * q : 96 * q + 96, :])
        for node in range(4):
            i = 4 * q + node
            value = tile(wide_s, i) + jnp.where(lane < 32, turn(below, -32 * node), 0.0)
            value = (value + jnp.where(lane % 32 == 0, turn(over, -i), 0.0)) * free[node]
            set_tile(image_s, i, value)
            set_tile(r, i, value - ritz_ref[...] * tile(s, i))
    first_nodes(r, r_layer, r_edge)
    flying = forward(r_layer, r_edge, r_ahead, r_side, r_corner)
    keep(early, 3, mm_nt(image_s[...], s[...]))
    keep(early, 4, mm_nt(image_s[...], p[...]))
    pack_gram(early, g)
    sum_1 = summed(g, from_core, half, from_plane, from_z, whole)
    next(sum_1)
    keep(late, 0, mm_nt(s[...], r[...]))
    keep(late, 3, mm_nt(image_s[...], r[...]))
    next(sum_1)
    keep(late, 1, mm_nt(p[...], r[...]))
    keep(late, 2, mm_nt(r[...], r[...]))
    finish(flying)
    corner, far_edge = far_edges(r_side[...], r_corner[...], top)
    put(columns, r, r_ahead, r_side[...], far_edge, top)
    products(columns, image, stencil_ref, coef)
    take(image, wide)
    next(sum_1)
    keep(late, 5, mm_nt(wide[...], ext(r, r_ahead, r_side, corner)))
    keep(late, 4, mm_nt(ext(p, p_ahead, p_side, p_corner_own), wide[...]))
    pack_gram(late, g_2)
    sum_2 = summed(g_2, from_core_2, half_2, from_plane_2, from_z_2, whole_2)
    next(sum_2)
    next(sum_1)
    next(sum_2)
    pack(r, r_pack)
    r_came[x] = r_pack[x]
    next(sum_1)
    next(sum_2)
    next(sum_1, None)

    b11, b12, b22, a11, a12, a22 = unpack_gram(whole)
    (d1, e1), (d2, e2) = diagonal(a11 + b11), diagonal(a22 + b22)
    b21 = pad(cut(b12).T)
    v1 = cut(sweep((a11 + b11) * d1 * e1))
    next(sum_2)
    z1 = mm(v1, jnp.concatenate([(a12 + b12) * d1 * e2, b11 * d1], 1))
    z12, y1 = cut(z1), z1[:, 128:]
    s2 = jnp.concatenate([(a22 + b22) * d2 * e2, b21 * d2], 1) - mm(z12.T, z1)
    v2 = cut(sweep(s2[:, :128]))
    next(sum_2)
    y2 = mm(v2, s2[:, 128:])
    u2 = mm(v2.T, y2)
    u1 = mm(v1.T, y1 - mm(z12, u2))
    u = jnp.concatenate([u1 * d1, u2 * d2], 0)
    next(sum_2, None)
    r_flying = exchange(r_pack, r_came)
    b13, b23, b33, a13, a23, a33 = unpack_gram(whole_2)
    d3, e3 = diagonal(a33 + b33)
    b31, b32 = pad(cut(b13).T), pad(cut(b23).T)
    z13 = mm(v1, (a13 + b13) * d1 * e3)
    z23 = mm(v2, (a23 + b23) * d2 * e3 - mm(z12.T, z13))
    z3 = jnp.concatenate([z13, z23], 0)
    s3 = jnp.concatenate([(a33 + b33) * d3 * e3, b31 * d3], 1) - mm(
        cut(z3).T, jnp.concatenate([z3, jnp.concatenate([y1, y2], 0)], 1)
    )
    v3 = cut(sweep(s3[:, :128]))
    h2 = mm(v2.T, z23)
    h1 = mm(v1.T, z13 - mm(z12, h2))
    own = jnp.where(lane == lax.broadcasted_iota(jnp.int32, (K, 128), 0), d3, 0.0)
    h = jnp.concatenate([h1 * -d1, h2 * -d2, own], 0)
    big = jnp.concatenate(
        [
            jnp.concatenate([cut(b11), cut(b12), cut(b13)], 1),
            jnp.concatenate([cut(b21), cut(b22), cut(b23)], 1),
            jnp.concatenate([cut(b31), cut(b32), cut(b33)], 1),
        ],
        0,
    )
    image_u = mm(big[:, : 2 * K], u)
    h_t = cut(h).T
    p = mm(h_t, jnp.concatenate([image_u, mm(big, h)], 1))
    p0, p1, p2 = mm(cut(u).T, image_u[: 2 * K]), p[:, :128], cut(p[:, 128:])
    w3 = mm(v3.T, mm(v3, s3[:, 128:]))
    small = p0 + mm(cut(p1).T, w3) + mm(cut(w3).T, p1 + mm(p2, w3))
    wt = cut(jnp.concatenate([u, jnp.zeros((K, 128), F32)], 0) + mm(cut(h), w3)).T
    ds, es = diagonal(small)
    rot_ref[...] = mm(cut(sweep(small * ds * es) * es), wt) * math.sqrt(UNKNOWNS)
    finish(r_flying)
    unpack(r_came, r_out)
    stores.append(pltpu.make_async_copy(r_out, r_hbm, local.at[9]))
    stores[2].start()
    for store in stores:
        store.wait()


def front(start, search, held, ids, kmat, ritz, moduli):
    def rows(*shape):
        return pltpu.VMEM(shape + (128,), F32)

    field = pltpu.VMEM((K, 1536), F32)
    return pl.pallas_call(
        front_kernel,
        out_shape=[jax.ShapeDtypeStruct((K, 288), F32)] + [jax.ShapeDtypeStruct((K, 1536), F32)] * 3,
        in_specs=[HBM] * 7,
        out_specs=[VMEM] + [HBM] * 3,
        scratch_shapes=[field] * 3
        + [rows(1152)] * 2
        + [pltpu.VMEM((n, 1, 128), jnp.int32) for n in (4, 3)]
        + [pltpu.VMEM(shape, F32) for shape in ((24, 24), (1, K), (1, 3), (K, 1))]
        + [pltpu.VMEM((96, 384), BF16)]
        + [field] * 4
        + [rows(K * 64)] * 2
        + [pltpu.VMEM((K, 17 * 128), F32)] * 2
        + [rows(6, K)] * 2
        + [rows(4, 296), rows(4, 288), rows(4, 288)] * 2
        + [rows(288)] * 3 + [rows(K)] * 3
        + [rows(288)] * 3 + [rows(K)] * 6
        + [rows(288), rows(K), rows(K)] * 2
        + [rows(64, 8), rows(32, 8), rows(32, 8), rows(15, 2, 8), rows(4, 2, 8), rows(64, 8)] * 2
        + [pltpu.SemaphoreType.DMA((10,)), pltpu.SemaphoreType.DMA((COPIES,)), pltpu.SemaphoreType.DMA((COPIES,))],
        compiler_params=pltpu.CompilerParams(vmem_limit_bytes=ROOM, collective_id=0, has_side_effects=True),
        name="front",
    )(start, search, held, ids, kmat, ritz, moduli)


def pack_gram(blocks, g):
    lane = lanes_of(K)
    for unit, index in enumerate((0, 1, 2, 4, 5)):
        beside = turn(blocks[3], 96 - 32 * unit) if unit < 3 else 0.0
        g[12 * unit : 12 * unit + 12] = jnp.where(lane < K, blocks[index], beside).reshape(12, 8, 128)
    g[60:64] = jnp.zeros((4, 8, 128), F32)


def unpack_gram(g):
    lane = lanes_of(K)
    units = [g[12 * unit : 12 * unit + 12].reshape(K, 128) for unit in range(5)]
    fourth = jnp.zeros((K, 128), F32)
    for n in range(3):
        fourth = jnp.where(lane // 32 == n, turn(units[n], 32 + 32 * n), fourth)
    units = [jnp.where(lane < K, unit, 0.0) for unit in units]
    return units[:3] + [fourth] + units[3:]


def rotate_kernel(rot_ref, s_hbm, r_hbm, p_hbm, block_ref, search_ref, s_ref, r_ref, p_ref, local):
    loads = [
        pltpu.make_async_copy(source, target, local.at[n])
        for n, (source, target) in enumerate(((s_hbm, s_ref), (r_hbm, r_ref), (p_hbm, p_ref)))
    ]
    for load in loads:
        load.start()
    rot = rot_ref[...]
    for load in loads:
        load.wait()
    for i in range(6):
        lanes = slice(256 * i, 256 * i + 256)
        tail = mm(rot[:, K:], jnp.concatenate([p_ref[:, lanes], r_ref[:, lanes]], 0))
        head = tail + mm(rot[:, :K], s_ref[:, lanes])
        for h in range(2):
            block_ref[pl.ds(2 * i + h, K, stride=12), :] = head[:, 128 * h : 128 * h + 128]
            search_ref[pl.ds(2 * i + h, K, stride=12), :] = tail[:, 128 * h : 128 * h + 128]


def rotate(rot, s, r, p):
    return pl.pallas_call(
        rotate_kernel,
        out_shape=[jax.ShapeDtypeStruct((1152, 128), F32)] * 2,
        in_specs=[VMEM] + [HBM] * 3,
        out_specs=[VMEM] * 2,
        scratch_shapes=[pltpu.VMEM((K, 1536), F32)] * 3 + [pltpu.SemaphoreType.DMA((3,))],
        compiler_params=pltpu.CompilerParams(vmem_limit_bytes=ROOM),
        name="rotate",
    )(rot, s, r, p)


def on_device(start_block, search_block, ritz_values, element_matrix, moduli, material_ids, held):
    shape = start_block.shape
    rot, s, r, p = front(
        start_block.reshape(1152, 128), search_block.reshape(1152, 128), held,
        material_ids, element_matrix, ritz_values.reshape(1, K), moduli.reshape(1, 3),
    )
    block, search = rotate(rot, s, r, p)
    return block.reshape(shape), search.reshape(shape)


def solution(mesh):
    split_field = P(None, None, None, "axial", "hoop")
    split_nodes = P(None, "axial", "hoop")
    in_specs = (split_field, split_field, P(), P(), P(), split_nodes, split_nodes)
    return jax.shard_map(
        on_device, mesh=mesh, in_specs=in_specs, out_specs=(split_field, split_field), check_vma=False
    )
```

```python
import functools
import math

import jax
import jax.numpy as jnp
from jax import lax
from jax.experimental import pallas as pl
from jax.experimental.pallas import tpu as pltpu
from jax.sharding import PartitionSpec as P

HI = lax.Precision.HIGHEST
MESH = pl.DeviceIdType.MESH
K = 96
F32 = jnp.float32
BF16 = jnp.bfloat16
VMEM = pl.BlockSpec(memory_space=pltpu.VMEM)
SMEM = pl.BlockSpec(memory_space=pltpu.SMEM)
HBM = pl.BlockSpec(memory_space=pltpu.HBM)
ROOM = 62 * 2**20
UNKNOWNS = 196608
UNROLL = 12
COPIES = 96
PLANE = [(dx, dy) for dx in (2, 1, 3, 0) for dy in (2, 1, 3, 0) if (dx, dy) != (0, 0)]


def sweep(block, factor=True):
    lane = lax.broadcasted_iota(jnp.int32, (8, 128), 1)
    sub = lax.broadcasted_iota(jnp.int32, (8, 128), 0)
    tiles = [block[8 * t : 8 * t + 8, :] for t in range(12)]

    def spread(value, at):
        return [jnp.broadcast_to(value[:, at + j : at + j + 1], (8, 128)) for j in range(4)]

    def pick(column, at):
        return jnp.broadcast_to(column[at : at + 1, :], (8, 128))

    def square(at):
        wide = spread(tiles[at // 8], at)
        return [[pick(wide[j], at % 8 + i) if j >= i else None for j in range(4)] for i in range(4)]

    found = []
    pivot = square(0)
    for group in range(24):
        p = 4 * group
        home, low = p // 8, p % 8
        below = range(home if low == 0 else home + 1, 12)
        cols = {t: spread(tiles[t], p) for t in below}
        (a00, a01, b00, b01), (_, a11, b10, b11), (_, _, c00, c01), (_, _, _, c11) = pivot
        ia = pl.reciprocal(a00 * a11 - a01 * a01)
        h00, h01, h11 = a11 * ia, -a01 * ia, a00 * ia
        x00, x01 = h00 * b00 + h01 * b10, h00 * b01 + h01 * b11
        x10, x11 = h01 * b00 + h11 * b10, h01 * b01 + h11 * b11
        s00 = c00 - (b00 * x00 + b10 * x10)
        s01 = c01 - (b00 * x01 + b10 * x11)
        s11 = c11 - (b01 * x01 + b11 * x11)
        ic = pl.reciprocal(s00 * s11 - s01 * s01)
        g00, g01, g11 = s11 * ic, -s01 * ic, s00 * ic

        def solve(f0, f1, f2, f3):
            u0 = f2 - (x00 * f0 + x10 * f1)
            u1 = f3 - (x01 * f0 + x11 * f1)
            n2 = g00 * u0 + g01 * u1
            n3 = g01 * u0 + g11 * u1
            n0 = (h00 * f0 + h01 * f1) - (x00 * n2 + x01 * n3)
            n1 = (h01 * f0 + h11 * f1) - (x10 * n2 + x11 * n3)
            return [n0, n1, n2, n3], u0, u1

        if group < 23:
            q = p + 4
            old = square(q)
            ahead = [[pick(cols[q // 8][i], q % 8 + j) for i in range(4)] for j in range(4)]
            factors = [solve(*ahead[j])[0] for j in range(4)]
            pivot = [
                [
                    old[i][j]
                    - ((ahead[i][0] * factors[j][0] + ahead[i][1] * factors[j][1])
                       + (ahead[i][2] * factors[j][2] + ahead[i][3] * factors[j][3]))
                    if j >= i else None
                    for j in range(4)
                ]
                for i in range(4)
            ]
        picked = (lane >= p) & (lane < p + 4)
        full = [jnp.where(picked, jnp.where(lane == p + j, 1.0, 0.0), pick(tiles[home], low + j)) for j in range(4)]
        new, u0, u1 = solve(*full)
        left = [jnp.where(lane < p + 4, f, 0.0) for f in full[:2]]
        y0, y1 = (jnp.where(lane < p + 4, u, 0.0) for u in (u0, u1))
        ra, rs = pl.reciprocal(a00), pl.reciprocal(s00)
        e1, e3 = a11 - a01 * a01 * ra, s11 - s01 * s01 * rs
        found.append(
            [
                left[0] * lax.rsqrt(a00),
                (left[1] - a01 * ra * left[0]) * lax.rsqrt(e1),
                y0 * lax.rsqrt(s00),
                (y1 - s01 * rs * y0) * lax.rsqrt(e3),
            ]
        )
        for t in below:
            c = cols[t]
            tiles[t] = jnp.where(picked, 0.0, tiles[t]) - (
                (c[0] * new[0] + c[1] * new[1]) + (c[2] * new[2] + c[3] * new[3])
            )
    out = []
    for t in range(12):
        eight = found[2 * t] + found[2 * t + 1]
        whole = eight[0]
        for s in range(1, 8):
            whole = jnp.where(sub == s, eight[s], whole)
        out.append(whole)
    return jnp.concatenate(out, 0)


def mm(a, b):
    return lax.dot_general(a, b, (((1,), (0,)), ((), ())), precision=HI, preferred_element_type=F32)


def diagonal(block):
    lane = lax.broadcasted_iota(jnp.int32, (K, 128), 1)
    row = lax.broadcasted_iota(jnp.int32, (K, 128), 0)
    only = jnp.where(lane == row, block, 0.0)
    down = jnp.sum(only, 1, keepdims=True)
    along = jnp.sum(only, 0, keepdims=True)
    return lax.rsqrt(down), lax.rsqrt(jnp.where(along == 0.0, 1.0, along))


def cut(block):
    return block[:, :K]


def pad(block):
    return jnp.concatenate([block, jnp.zeros((block.shape[0], 128 - block.shape[1]), F32)], 1)


def mm_nt(a, b):
    return lax.dot_general(a, b, (((1,), (1,)), ((), ())), precision=HI, preferred_element_type=F32)


def split(x):
    high = x.astype(BF16)
    rest = x - high.astype(F32)
    middle = rest.astype(BF16)
    low = (rest - middle.astype(F32)).astype(BF16)
    return high, middle, low


def stencil(kmat):
    def rows_of(shape, axis):
        at = lax.broadcasted_iota(jnp.int32, shape, axis)
        low, high = at % 8, at // 8
        dh, high = high % 2, high // 2
        return low // 3, low % 3, dh, high % 3, high // 3, low < 6

    def columns_of(shape, axis):
        at = lax.broadcasted_iota(jnp.int32, shape, axis)
        low, high = at % 8, at // 8
        return low // 3, low % 3, high // 4, high % 4, low < 6

    da, q, dh, _, dr, real = rows_of((96, 24), 0)
    corner = lax.broadcasted_iota(jnp.int32, (96, 24), 1)
    pick = jnp.where(real & (corner == 3 * (4 * dr + 2 * da + dh) + q), 1.0, 0.0)
    picked = mm(pick, kmat)
    layer = rows_of((96, 64), 0)[3]
    node = columns_of((96, 64), 1)[3]
    total = jnp.zeros((96, 64), F32)
    for dr in range(2):
        da, q, dh, _, real = columns_of((24, 64), 1)
        corner = lax.broadcasted_iota(jnp.int32, (24, 64), 0)
        place = jnp.where(real & (corner == 3 * (4 * dr + 2 * da + dh) + q), 1.0, 0.0)
        total = total + jnp.where(node == layer + dr, mm(picked, place), 0.0)
    high, middle, low = split(total)
    return jnp.concatenate([high, high, high, middle, middle, low], 1)


def lanes_of(rows):
    return lax.broadcasted_iota(jnp.int32, (rows, 128), 1)


def turn(x, by):
    return pltpu.roll(x, by % 128, 1) if by % 128 else x


def swap(tiles):
    lane = lanes_of(tiles[0].shape[0])
    front, even = lane < 64, (lane // 32) % 2 == 0
    a, b, c, d = tiles
    a, c = jnp.where(front, a, turn(c, 64)), jnp.where(front, turn(a, 64), c)
    b, d = jnp.where(front, b, turn(d, 64)), jnp.where(front, turn(b, 64), d)
    a, b = jnp.where(even, a, turn(b, 32)), jnp.where(even, turn(a, 96), b)
    c, d = jnp.where(even, c, turn(d, 32)), jnp.where(even, turn(c, 96), d)
    return a, b, c, d


def tile(ref, i):
    return ref[:, 128 * i : 128 * i + 128]


def set_tile(ref, i, value):
    ref[:, 128 * i : 128 * i + 128] = value


def pack(field_ref, pack_ref):
    for q in range(3):
        for to, value in enumerate(swap([tile(field_ref, 4 * q + r) for r in range(4)])):
            pack_ref[to, 96 * q : 96 * q + 96, :] = value


def unpack(came_ref, field_ref):
    for q in range(3):
        for r, value in enumerate(swap([came_ref[j, 96 * q : 96 * q + 96, :] for j in range(4)])):
            set_tile(field_ref, 4 * q + r, value)


def first_nodes(field_ref, layer_ref, edge_ref):
    lane = lanes_of(K)
    edge = jnp.zeros((K, 128), F32)
    for q in range(3):
        layer = jnp.zeros((K, 128), F32)
        for r in range(4):
            value = tile(field_ref, 4 * q + r)
            layer = jnp.where(lane // 32 == r, turn(value, 32 * r), layer)
            edge = jnp.where(lane % 32 == 4 * q + r, turn(value, 4 * q + r), edge)
        layer_ref[96 * q : 96 * q + 96, :] = layer
    edge_ref[...] = edge


def put(columns_ref, field_ref, layer_ref, edge, far_edge, top):
    lane = lanes_of(K)
    for q in range(3):
        for r in range(4):
            i = 4 * q + r
            near = tile(field_ref, i)
            ahead = jnp.where(top, 0.0, turn(layer_ref[96 * q : 96 * q + 96, :], 32 * (3 - r)))
            far = jnp.where(lane < 96, turn(near, 96), ahead)
            for da, (value, side) in enumerate(((near, edge), (far, far_edge))):
                at = 8 * r + 3 * da + q
                columns_ref[pl.ds(at, K, stride=64), :] = value
                moved = jnp.where(lane % 32 == 31, turn(side, 31 - i), turn(value, 127))
                columns_ref[pl.ds(32 + at, K, stride=64), :] = moved


def far_edges(edge, corner, top):
    lane = lanes_of(K)
    corner = jnp.where(top, 0.0, jnp.where(lane < 96, 0.0, turn(corner, 96)))
    return corner, jnp.where(lane < 96, turn(edge, 96), corner)


def products(columns_ref, image_ref, stencil_ref, coef):
    weights = stencil_ref[...]
    coef = [jnp.broadcast_to(coef[r : r + 1], (8, 128)) for r in range(3)]
    wide = 8

    def step(group, carry):
        base = pl.multiple_of(64 * wide * group, 64 * wide)
        some = columns_ref[pl.ds(base, 64 * wide), :]
        high, middle, low = split(jnp.concatenate([some[64 * c : 64 * c + 64] for c in range(wide)], 1))
        stack = jnp.concatenate([high, middle, low, high, middle, high], 0)
        terms = jnp.dot(weights, stack, preferred_element_type=F32)
        for c in range(wide):
            term = terms[:, 128 * c : 128 * c + 128]

            def part(dr, r, dh):
                at = 8 * ((dr * 3 + r) * 2 + dh)
                return term[at : at + 8] * coef[r]

            values = []
            for dh in range(2):
                for node in range(4):
                    parts = [part(dr, node - dr, dh) for dr in range(2) if 0 <= node - dr < 3]
                    values.append(parts[0] if len(parts) == 1 else parts[0] + parts[1])
            image_ref[pl.ds(base + 64 * c, 64), :] = jnp.concatenate(values, 0)
        return carry

    lax.fori_loop(0, K // wide, step, 0, unroll=UNROLL)


def take(image_ref, wide_ref):
    lane = lanes_of(K)
    over, far_over = jnp.zeros((K, 128), F32), jnp.zeros((K, 128), F32)
    for q in range(3):
        layer = jnp.zeros((K, 128), F32)
        for r in range(4):
            i = 4 * q + r
            at = 8 * r + q

            def shifted_sum(at):
                second = image_ref[pl.ds(32 + at, K, stride=64), :]
                first = image_ref[pl.ds(at, K, stride=64), :]
                return first + jnp.where(lane % 32 == 0, 0.0, turn(second, 1)), turn(second, i - 31)

            near, out = shifted_sum(at)
            far, far_out = shifted_sum(at + 3)
            over = jnp.where(lane % 32 == i, out, over)
            far_over = jnp.where(lane % 32 == i, far_out, far_over)
            set_tile(wide_ref, i, near + jnp.where(lane < 32, 0.0, turn(far, 32)))
            layer = jnp.where(lane // 32 == r, turn(far, 32 * (r - 3)), layer)
        set_tile(wide_ref, 12 + q, layer)
    set_tile(wide_ref, 15, over + jnp.where(lane < 32, 0.0, turn(far_over, 32)))
    set_tile(wide_ref, 16, jnp.where(lane < 96, 0.0, far_over))


def front_kernel(
    start_hbm, search_hbm, held_hbm, ids_hbm, kmat_hbm, ritz_hbm, moduli_hbm,
    rot_ref, s_hbm, r_hbm, p_hbm,
    s_out, r_out, p_out,
    start_in, search_in, held_ref, ids_ref, kmat_ref, ritz_row, moduli_ref, ritz_ref, stencil_ref, s, r, p, image_s, columns, image, wide, wide_s, early, late, hold,
    s_pack, p_pack, r_pack, s_came, p_came, r_came,
    s_layer, r_layer, p_layer, s_edge, r_edge, p_edge,
    s_ahead, r_ahead, p_ahead, s_side, r_side, p_side, s_corner, r_corner, p_corner,
    back, back_over, back_corner, back_came, over_came, corner_came,
    g, from_core, half, from_plane, from_z, whole,
    g_2, from_core_2, half_2, from_plane_2, from_z_2, whole_2,
    local, send, recv,
):
    axial, hoop = lax.axis_index("axial"), lax.axis_index("hoop")
    z, x = axial // 4, axial % 4
    y, core = hoop // 2, hoop % 2
    top, bottom = z == 3, z == 0
    lane = lanes_of(K)

    def at(z, x, y, core):
        return (z * 4 + x, y * 2 + core)

    def around(dz, ds):
        sector = (hoop * 4 + x + ds + 32) % 32
        return ((z + dz + 4) % 4 * 4 + sector % 4, sector // 4)

    peers = {
        "core": [at(z, x, y, 1 - core)],
        "plane": [at(z, (x + dx) % 4, (y + dy) % 4, core) for dx, dy in PLANE],
        "z": [at((z + d) % 4, x, y, core) for d in (1, 2, 3)],
        "hoop": [around(0, 1), around(0, -1), around(1, 1), around(-1, -1)],
    }
    pairs = (
        (start_hbm, start_in), (search_hbm, search_in), (held_hbm, held_ref), (ids_hbm, ids_ref),
        (kmat_hbm, kmat_ref), (ritz_hbm, ritz_row), (moduli_hbm, moduli_ref),
    )
    loads = [pltpu.make_async_copy(source, target, local.at[n]) for n, (source, target) in enumerate(pairs)]
    for load in loads:
        load.start()
    barrier = pltpu.get_barrier_semaphore()
    count = 0
    for group in peers.values():
        for peer in group:
            pl.semaphore_signal(barrier, inc=1, device_id=peer, device_id_type=MESH)
            count += 1
    used = [0]

    def copy(source, target, peer):
        index = used[0]
        used[0] += 1
        made = pltpu.make_async_remote_copy(
            src_ref=source, dst_ref=target, send_sem=send.at[index], recv_sem=recv.at[index],
            device_id=peer, device_id_type=MESH,
        )
        made.start()
        return made

    def finish(copies):
        for made in copies:
            made.wait()

    def exchange(pack_ref, came_ref):
        copies = []
        for d in (2, 1, 3):
            copies.append(copy(pack_ref.at[(x + d) % 4], came_ref.at[x], at(z, (x + d) % 4, y, core)))
        return copies

    def forward(layer, edge, ahead, side, corner):
        return [
            copy(layer, ahead, around(-1, 0)),
            copy(edge, side, around(0, -1)),
            copy(edge, corner, around(-1, -1)),
        ]

    def summed(g, from_core, half, from_plane, from_z, whole):
        copies = [copy(g.at[pl.ds((1 - core) * 32, 32)], from_core, peers["core"][0])]
        yield
        finish(copies)
        half[...] = g[pl.ds(core * 32, 32)] + from_core[...]
        copies = []
        for n, ((dx, dy), peer) in enumerate(zip(PLANE, peers["plane"])):
            part = ((x + dx) % 4 * 4 + (y + dy) % 4) * 2
            copies.append(copy(half.at[pl.ds(part, 2)], from_plane.at[n], peer))
        yield
        finish(copies)
        parts = [half[pl.ds((x * 4 + y) * 2, 2)]] + [from_plane[n] for n in range(15)]
        while len(parts) > 1:
            parts = [parts[n] + parts[n + 1] for n in range(0, len(parts), 2)]
        from_z[z] = parts[0]
        copies = [copy(from_z.at[z], from_z.at[z], peer) for peer in peers["z"]]
        yield
        finish(copies)
        first = core * 32 + (x * 4 + y) * 2
        whole[pl.ds(first, 2)] = (from_z[0] + from_z[1]) + (from_z[2] + from_z[3])
        part = whole.at[pl.ds(first, 2)]
        copies = [copy(part, part, peer) for peer in peers["plane"]]
        yield
        finish(copies)
        part = whole.at[pl.ds(core * 32, 32)]
        copies = [copy(part, part, peers["core"][0])]
        yield
        finish(copies)

    for load in loads[2:]:
        load.wait()
    coef = []
    for layer in range(3):
        ids = ids_ref[layer]
        total = jnp.zeros((1, 128), F32)
        for material in range(3):
            total = total + jnp.where(ids == material, moduli_ref[0:1, material : material + 1], 0.0)
        coef.append(total)
    free = [(1 - held_ref[node]).astype(F32) for node in range(4)]
    ritz = jnp.broadcast_to(jnp.concatenate([ritz_row[...], jnp.zeros((1, 32), F32)], 1), (K, 128))
    ritz_ref[...] = jnp.sum(jnp.where(lane == lax.broadcasted_iota(jnp.int32, (K, 128), 0), ritz, 0.0), 1, keepdims=True)
    row = lax.broadcasted_iota(jnp.int32, (8, 128), 0)
    notes = []
    for node in range(4):
        note = jnp.where(row == 0, free[node], 0.0)
        notes.append(jnp.where(row == 1, coef[node], note) if node < 3 else note)
    for to, value in enumerate(swap(notes)):
        s_pack[to, 288:296, :] = value

    def mask_in(source, field_out):
        for i in range(12):
            set_tile(field_out, i, source[pl.ds(i, K, stride=12), :] * free[i % 4])

    loads[0].wait()
    mask_in(start_in, s_out)
    pack(s_out, s_pack)
    pl.semaphore_wait(barrier, count)
    flying = exchange(s_pack, s_came)
    s_came[x] = s_pack[x]
    stencil_ref[...] = stencil(kmat_ref[...])
    zero = jnp.zeros((K, 128), F32)
    for high in range(8):
        for low in (6, 7):
            columns[pl.ds(8 * high + low, K, stride=64), :] = zero
    loads[1].wait()
    mask_in(search_in, p_out)
    pack(p_out, p_pack)
    p_flying = exchange(p_pack, p_came)
    p_came[x] = p_pack[x]
    stores = [
        pltpu.make_async_copy(s_out, s_hbm, local.at[7]),
        pltpu.make_async_copy(p_out, p_hbm, local.at[8]),
    ]
    for store in stores:
        store.start()
    finish(flying)

    def stage(work):
        pl.when(axial >= 0)(work)

    def keep(blocks, index, value):
        blocks[index, :, 0:K] = value

    notes = swap([s_came[j, 288:296, :] for j in range(4)])
    free = [note[0:1] for note in notes]
    coef = jnp.concatenate([note[1:2] for note in notes[:3]], 0)

    @stage
    def _():
        unpack(s_came, s)
        first_nodes(s, s_layer, s_edge)

    flying = forward(s_layer, s_edge, s_ahead, s_side, s_corner)

    @stage
    def _():
        keep(early, 0, mm_nt(s[...], s[...]))

    finish(p_flying)

    @stage
    def _():
        unpack(p_came, p)
        first_nodes(p, p_layer, p_edge)

    p_flying = forward(p_layer, p_edge, p_ahead, p_side, p_corner)

    @stage
    def _():
        keep(early, 1, mm_nt(s[...], p[...]))
        keep(early, 2, mm_nt(p[...], p[...]))

    def ext(field, ahead, side, corner):
        layers = [jnp.where(top, 0.0, ahead[96 * q : 96 * q + 96, :]) for q in range(3)]
        return jnp.concatenate([field[...]] + layers + [side[...], far_edges(side[...], corner[...], top)[0]], 1)

    def operate(field, ahead, side, corner, result):
        put(columns, field, ahead, side[...], far_edges(side[...], corner[...], top)[1], top)
        products(columns, image, stencil_ref, coef)
        take(image, result)

    finish(flying)

    @stage
    def _():
        operate(s, s_ahead, s_side, s_corner, wide_s)
        for q in range(3):
            back[96 * q : 96 * q + 96, :] = tile(wide_s, 12 + q)
        back_over[...] = tile(wide_s, 15)
        back_corner[...] = tile(wide_s, 16)

    flying = [
        copy(back, back_came, around(1, 0)),
        copy(back_over, over_came, around(0, 1)),
        copy(back_corner, corner_came, around(1, 1)),
    ]

    finish(p_flying)

    @stage
    def _():
        operate(p, p_ahead, p_side, p_corner, wide)
        keep(early, 5, mm_nt(wide[...], ext(p, p_ahead, p_side, p_corner)))

    finish(flying)

    @stage
    def _():
        over = over_came[...] + jnp.where(bottom, 0.0, jnp.where(lane < 32, turn(corner_came[...], 32), 0.0))
        for q in range(3):
            below = jnp.where(bottom, 0.0, back_came[96 * q : 96 * q + 96, :])
            for node in range(4):
                i = 4 * q + node
                value = tile(wide_s, i) + jnp.where(lane < 32, turn(below, -32 * node), 0.0)
                value = (value + jnp.where(lane % 32 == 0, turn(over, -i), 0.0)) * free[node]
                set_tile(image_s, i, value)
                set_tile(r, i, value - ritz_ref[...] * tile(s, i))
        first_nodes(r, r_layer, r_edge)

    flying = forward(r_layer, r_edge, r_ahead, r_side, r_corner)

    @stage
    def _():
        keep(early, 3, mm_nt(image_s[...], s[...]))
        keep(early, 4, mm_nt(image_s[...], p[...]))
        pack_gram(early, g)

    sum_1 = summed(g, from_core, half, from_plane, from_z, whole)
    next(sum_1)

    @stage
    def _():
        keep(late, 0, mm_nt(s[...], r[...]))
        keep(late, 3, mm_nt(image_s[...], r[...]))

    next(sum_1)

    @stage
    def _():
        keep(late, 1, mm_nt(p[...], r[...]))
        keep(late, 2, mm_nt(r[...], r[...]))
        pack(r, r_pack)

    finish(flying)

    @stage
    def _():
        operate(r, r_ahead, r_side, r_corner, wide)

    next(sum_1)

    @stage
    def _():
        keep(late, 5, mm_nt(wide[...], ext(r, r_ahead, r_side, r_corner)))
        keep(late, 4, mm_nt(ext(p, p_ahead, p_side, p_corner), wide[...]))
        pack_gram(late, g_2)

    sum_2 = summed(g_2, from_core_2, half_2, from_plane_2, from_z_2, whole_2)
    next(sum_2)
    next(sum_1)
    next(sum_2)
    next(sum_1)
    next(sum_2)
    next(sum_1, None)

    @stage
    def _():
        b11, _, _, a11, _, _ = unpack_gram(whole)
        d1, e1 = diagonal(a11 + b11)
        hold[0] = sweep((a11 + b11) * d1 * e1)

    next(sum_2)

    @stage
    def _():
        b11, b12, b22, a11, a12, a22 = unpack_gram(whole)
        (d1, e1), (d2, e2) = diagonal(a11 + b11), diagonal(a22 + b22)
        z1 = mm(cut(hold[0]), jnp.concatenate([(a12 + b12) * d1 * e2, b11 * d1], 1))
        s2 = jnp.concatenate([(a22 + b22) * d2 * e2, pad(cut(b12).T) * d2], 1) - mm(cut(z1).T, z1)
        hold[1], hold[2] = z1[:, :128], z1[:, 128:]
        hold[3] = sweep(s2[:, :128])
        hold[4] = s2[:, 128:]

    next(sum_2)

    @stage
    def _():
        y2 = mm(cut(hold[3]), hold[4])
        u2 = mm(cut(hold[3]).T, y2)
        hold[4], hold[5] = y2, u2
        hold[6] = mm(cut(hold[0]).T, hold[2] - mm(cut(hold[1]), u2))

    next(sum_2, None)

    @stage
    def _():
        b11, _, b22, a11, _, a22 = unpack_gram(whole)
        b13, b23, b33, a13, a23, a33 = unpack_gram(whole_2)
        d1, d2, (d3, e3) = diagonal(a11 + b11)[0], diagonal(a22 + b22)[0], diagonal(a33 + b33)
        z13 = mm(cut(hold[0]), (a13 + b13) * d1 * e3)
        z23 = mm(cut(hold[3]), (a23 + b23) * d2 * e3 - mm(cut(hold[1]).T, z13))
        z3 = jnp.concatenate([z13, z23], 0)
        s3 = jnp.concatenate([(a33 + b33) * d3 * e3, pad(cut(b13).T) * d3], 1) - mm(
            cut(z3).T, jnp.concatenate([z3, jnp.concatenate([hold[2], hold[4]], 0)], 1)
        )
        hold[7], hold[8], hold[9], hold[10] = z13, z23, s3[:, :128], s3[:, 128:]

    r_flying = exchange(r_pack, r_came)
    r_came[x] = r_pack[x]

    @stage
    def _():
        b11, b12, b22, a11, _, a22 = unpack_gram(whole)
        b13, b23, b33, _, _, a33 = unpack_gram(whole_2)
        d1, d2, d3 = (diagonal(total)[0] for total in (a11 + b11, a22 + b22, a33 + b33))
        v3 = cut(sweep(hold[9]))
        u = jnp.concatenate([hold[6] * d1, hold[5] * d2], 0)
        h2 = mm(cut(hold[3]).T, hold[8])
        h1 = mm(cut(hold[0]).T, hold[7] - mm(cut(hold[1]), h2))
        own = jnp.where(lane == lax.broadcasted_iota(jnp.int32, (K, 128), 0), d3, 0.0)
        h = jnp.concatenate([h1 * -d1, h2 * -d2, own], 0)
        big = jnp.concatenate(
            [
                jnp.concatenate([cut(b11), cut(b12), cut(b13)], 1),
                jnp.concatenate([cut(b12).T, cut(b22), cut(b23)], 1),
                jnp.concatenate([cut(b13).T, cut(b23).T, cut(b33)], 1),
            ],
            0,
        )
        image_u = mm(big[:, : 2 * K], u)
        both = mm(cut(h).T, jnp.concatenate([image_u, mm(big, h)], 1))
        p0, p1, p2 = mm(cut(u).T, image_u[: 2 * K]), both[:, :128], cut(both[:, 128:])
        w3 = mm(v3.T, mm(v3, hold[10]))
        small = p0 + mm(cut(p1).T, w3) + mm(cut(w3).T, p1 + mm(p2, w3))
        wt = cut(jnp.concatenate([u, jnp.zeros((K, 128), F32)], 0) + mm(cut(h), w3)).T
        ds, es = diagonal(small)
        rot_ref[...] = mm(cut(sweep(small * ds * es) * es), wt) * math.sqrt(UNKNOWNS)

    finish(r_flying)
    unpack(r_came, r_out)
    stores.append(pltpu.make_async_copy(r_out, r_hbm, local.at[9]))
    stores[2].start()
    for store in stores:
        store.wait()


def front(start, search, held, ids, kmat, ritz, moduli):
    def rows(*shape):
        return pltpu.VMEM(shape + (128,), F32)

    field = pltpu.VMEM((K, 1536), F32)
    return pl.pallas_call(
        front_kernel,
        out_shape=[jax.ShapeDtypeStruct((K, 288), F32)] + [jax.ShapeDtypeStruct((K, 1536), F32)] * 3,
        in_specs=[HBM] * 7,
        out_specs=[VMEM] + [HBM] * 3,
        scratch_shapes=[field] * 3
        + [rows(1152)] * 2
        + [pltpu.VMEM((n, 1, 128), jnp.int32) for n in (4, 3)]
        + [pltpu.VMEM(shape, F32) for shape in ((24, 24), (1, K), (1, 3), (K, 1))]
        + [pltpu.VMEM((96, 384), BF16)]
        + [field] * 4
        + [rows(K * 64)] * 2
        + [pltpu.VMEM((K, 17 * 128), F32)] * 2
        + [rows(6, K)] * 2 + [rows(11, K)]
        + [rows(4, 296), rows(4, 288), rows(4, 288)] * 2
        + [rows(288)] * 3 + [rows(K)] * 3
        + [rows(288)] * 3 + [rows(K)] * 6
        + [rows(288), rows(K), rows(K)] * 2
        + [rows(64, 8), rows(32, 8), rows(32, 8), rows(15, 2, 8), rows(4, 2, 8), rows(64, 8)] * 2
        + [pltpu.SemaphoreType.DMA((10,)), pltpu.SemaphoreType.DMA((COPIES,)), pltpu.SemaphoreType.DMA((COPIES,))],
        compiler_params=pltpu.CompilerParams(vmem_limit_bytes=ROOM, collective_id=0, has_side_effects=True),
        name="front",
    )(start, search, held, ids, kmat, ritz, moduli)


def pack_gram(blocks, g):
    lane = lanes_of(K)
    for unit, index in enumerate((0, 1, 2, 4, 5)):
        beside = turn(blocks[3], 96 - 32 * unit) if unit < 3 else 0.0
        g[12 * unit : 12 * unit + 12] = jnp.where(lane < K, blocks[index], beside).reshape(12, 8, 128)
    g[60:64] = jnp.zeros((4, 8, 128), F32)


def unpack_gram(g):
    lane = lanes_of(K)
    units = [g[12 * unit : 12 * unit + 12].reshape(K, 128) for unit in range(5)]
    fourth = jnp.zeros((K, 128), F32)
    for n in range(3):
        fourth = jnp.where(lane // 32 == n, turn(units[n], 32 + 32 * n), fourth)
    units = [jnp.where(lane < K, unit, 0.0) for unit in units]
    return units[:3] + [fourth] + units[3:]


def rotate_kernel(rot_ref, s_hbm, r_hbm, p_hbm, block_ref, search_ref, s_ref, r_ref, p_ref, local):
    loads = [
        pltpu.make_async_copy(source, target, local.at[n])
        for n, (source, target) in enumerate(((s_hbm, s_ref), (r_hbm, r_ref), (p_hbm, p_ref)))
    ]
    for load in loads:
        load.start()
    rot = rot_ref[...]
    for load in loads:
        load.wait()
    for i in range(6):
        lanes = slice(256 * i, 256 * i + 256)
        tail = mm(rot[:, K:], jnp.concatenate([p_ref[:, lanes], r_ref[:, lanes]], 0))
        head = tail + mm(rot[:, :K], s_ref[:, lanes])
        for h in range(2):
            block_ref[pl.ds(2 * i + h, K, stride=12), :] = head[:, 128 * h : 128 * h + 128]
            search_ref[pl.ds(2 * i + h, K, stride=12), :] = tail[:, 128 * h : 128 * h + 128]


def rotate(rot, s, r, p):
    return pl.pallas_call(
        rotate_kernel,
        out_shape=[jax.ShapeDtypeStruct((1152, 128), F32)] * 2,
        in_specs=[VMEM] + [HBM] * 3,
        out_specs=[VMEM] * 2,
        scratch_shapes=[pltpu.VMEM((K, 1536), F32)] * 3 + [pltpu.SemaphoreType.DMA((3,))],
        compiler_params=pltpu.CompilerParams(vmem_limit_bytes=ROOM),
        name="rotate",
    )(rot, s, r, p)


def on_device(start_block, search_block, ritz_values, element_matrix, moduli, material_ids, held):
    shape = start_block.shape
    rot, s, r, p = front(
        start_block.reshape(1152, 128), search_block.reshape(1152, 128), held,
        material_ids, element_matrix, ritz_values.reshape(1, K), moduli.reshape(1, 3),
    )
    block, search = rotate(rot, s, r, p)
    return block.reshape(shape), search.reshape(shape)


def solution(mesh):
    split_field = P(None, None, None, "axial", "hoop")
    split_nodes = P(None, "axial", "hoop")
    in_specs = (split_field, split_field, P(), P(), P(), split_nodes, split_nodes)
    return jax.shard_map(
        on_device, mesh=mesh, in_specs=in_specs, out_specs=(split_field, split_field), check_vma=False
    )
```

```python
import functools
import math

import jax
import jax.numpy as jnp
from jax import lax
from jax.experimental import pallas as pl
from jax.experimental.pallas import tpu as pltpu
from jax.sharding import PartitionSpec as P

HI = lax.Precision.HIGHEST
MESH = pl.DeviceIdType.MESH
K = 96
F32 = jnp.float32
BF16 = jnp.bfloat16
VMEM = pl.BlockSpec(memory_space=pltpu.VMEM)
SMEM = pl.BlockSpec(memory_space=pltpu.SMEM)
HBM = pl.BlockSpec(memory_space=pltpu.HBM)
ROOM = 62 * 2**20
UNKNOWNS = 196608
UNROLL = 12
COPIES = 96
PLANE = [(dx, dy) for dx in (2, 1, 3, 0) for dy in (2, 1, 3, 0) if (dx, dy) != (0, 0)]


def sweep(block, factor=True):
    lane = lax.broadcasted_iota(jnp.int32, (8, 128), 1)
    sub = lax.broadcasted_iota(jnp.int32, (8, 128), 0)
    tiles = [block[8 * t : 8 * t + 8, :] for t in range(12)]

    def spread(value, at):
        return [jnp.broadcast_to(value[:, at + j : at + j + 1], (8, 128)) for j in range(4)]

    def pick(column, at):
        return jnp.broadcast_to(column[at : at + 1, :], (8, 128))

    def square(at):
        wide = spread(tiles[at // 8], at)
        return [[pick(wide[j], at % 8 + i) if j >= i else None for j in range(4)] for i in range(4)]

    found = []
    pivot = square(0)
    for group in range(24):
        p = 4 * group
        home, low = p // 8, p % 8
        below = range(home if low == 0 else home + 1, 12)
        cols = {t: spread(tiles[t], p) for t in below}
        (a00, a01, b00, b01), (_, a11, b10, b11), (_, _, c00, c01), (_, _, _, c11) = pivot
        ia = pl.reciprocal(a00 * a11 - a01 * a01)
        h00, h01, h11 = a11 * ia, -a01 * ia, a00 * ia
        x00, x01 = h00 * b00 + h01 * b10, h00 * b01 + h01 * b11
        x10, x11 = h01 * b00 + h11 * b10, h01 * b01 + h11 * b11
        s00 = c00 - (b00 * x00 + b10 * x10)
        s01 = c01 - (b00 * x01 + b10 * x11)
        s11 = c11 - (b01 * x01 + b11 * x11)
        ic = pl.reciprocal(s00 * s11 - s01 * s01)
        g00, g01, g11 = s11 * ic, -s01 * ic, s00 * ic

        def solve(f0, f1, f2, f3):
            u0 = f2 - (x00 * f0 + x10 * f1)
            u1 = f3 - (x01 * f0 + x11 * f1)
            n2 = g00 * u0 + g01 * u1
            n3 = g01 * u0 + g11 * u1
            n0 = (h00 * f0 + h01 * f1) - (x00 * n2 + x01 * n3)
            n1 = (h01 * f0 + h11 * f1) - (x10 * n2 + x11 * n3)
            return [n0, n1, n2, n3], u0, u1

        if group < 23:
            q = p + 4
            old = square(q)
            ahead = [[pick(cols[q // 8][i], q % 8 + j) for i in range(4)] for j in range(4)]
            factors = [solve(*ahead[j])[0] for j in range(4)]
            pivot = [
                [
                    old[i][j]
                    - ((ahead[i][0] * factors[j][0] + ahead[i][1] * factors[j][1])
                       + (ahead[i][2] * factors[j][2] + ahead[i][3] * factors[j][3]))
                    if j >= i else None
                    for j in range(4)
                ]
                for i in range(4)
            ]
        picked = (lane >= p) & (lane < p + 4)
        full = [jnp.where(picked, jnp.where(lane == p + j, 1.0, 0.0), pick(tiles[home], low + j)) for j in range(4)]
        new, u0, u1 = solve(*full)
        left = [jnp.where(lane < p + 4, f, 0.0) for f in full[:2]]
        y0, y1 = (jnp.where(lane < p + 4, u, 0.0) for u in (u0, u1))
        ra, rs = pl.reciprocal(a00), pl.reciprocal(s00)
        e1, e3 = a11 - a01 * a01 * ra, s11 - s01 * s01 * rs
        found.append(
            [
                left[0] * lax.rsqrt(a00),
                (left[1] - a01 * ra * left[0]) * lax.rsqrt(e1),
                y0 * lax.rsqrt(s00),
                (y1 - s01 * rs * y0) * lax.rsqrt(e3),
            ]
        )
        for t in below:
            c = cols[t]
            tiles[t] = jnp.where(picked, 0.0, tiles[t]) - (
                (c[0] * new[0] + c[1] * new[1]) + (c[2] * new[2] + c[3] * new[3])
            )
    out = []
    for t in range(12):
        eight = found[2 * t] + found[2 * t + 1]
        whole = eight[0]
        for s in range(1, 8):
            whole = jnp.where(sub == s, eight[s], whole)
        out.append(whole)
    return jnp.concatenate(out, 0)


def mm(a, b):
    return lax.dot_general(a, b, (((1,), (0,)), ((), ())), precision=HI, preferred_element_type=F32)


def diagonal(block):
    lane = lax.broadcasted_iota(jnp.int32, (K, 128), 1)
    row = lax.broadcasted_iota(jnp.int32, (K, 128), 0)
    only = jnp.where(lane == row, block, 0.0)
    down = jnp.sum(only, 1, keepdims=True)
    along = jnp.sum(only, 0, keepdims=True)
    return lax.rsqrt(down), lax.rsqrt(jnp.where(along == 0.0, 1.0, along))


def cut(block):
    return block[:, :K]


def pad(block):
    return jnp.concatenate([block, jnp.zeros((block.shape[0], 128 - block.shape[1]), F32)], 1)


def mm_nt(a, b):
    return lax.dot_general(a, b, (((1,), (1,)), ((), ())), precision=HI, preferred_element_type=F32)


def split(x):
    high = x.astype(BF16)
    rest = x - high.astype(F32)
    middle = rest.astype(BF16)
    low = (rest - middle.astype(F32)).astype(BF16)
    return high, middle, low


def stencil(kmat):
    def rows_of(shape, axis):
        at = lax.broadcasted_iota(jnp.int32, shape, axis)
        low, high = at % 8, at // 8
        dh, high = high % 2, high // 2
        return low // 3, low % 3, dh, high % 3, high // 3, low < 6

    def columns_of(shape, axis):
        at = lax.broadcasted_iota(jnp.int32, shape, axis)
        low, high = at % 8, at // 8
        return low // 3, low % 3, high // 4, high % 4, low < 6

    da, q, dh, _, dr, real = rows_of((96, 24), 0)
    corner = lax.broadcasted_iota(jnp.int32, (96, 24), 1)
    pick = jnp.where(real & (corner == 3 * (4 * dr + 2 * da + dh) + q), 1.0, 0.0)
    picked = mm(pick, kmat)
    layer = rows_of((96, 64), 0)[3]
    node = columns_of((96, 64), 1)[3]
    total = jnp.zeros((96, 64), F32)
    for dr in range(2):
        da, q, dh, _, real = columns_of((24, 64), 1)
        corner = lax.broadcasted_iota(jnp.int32, (24, 64), 0)
        place = jnp.where(real & (corner == 3 * (4 * dr + 2 * da + dh) + q), 1.0, 0.0)
        total = total + jnp.where(node == layer + dr, mm(picked, place), 0.0)
    high, middle, low = split(total)
    return jnp.concatenate([high, high, high, middle, middle, low], 1)


def lanes_of(rows):
    return lax.broadcasted_iota(jnp.int32, (rows, 128), 1)


def turn(x, by):
    return pltpu.roll(x, by % 128, 1) if by % 128 else x


def swap(tiles):
    lane = lanes_of(tiles[0].shape[0])
    front, even = lane < 64, (lane // 32) % 2 == 0
    a, b, c, d = tiles
    a, c = jnp.where(front, a, turn(c, 64)), jnp.where(front, turn(a, 64), c)
    b, d = jnp.where(front, b, turn(d, 64)), jnp.where(front, turn(b, 64), d)
    a, b = jnp.where(even, a, turn(b, 32)), jnp.where(even, turn(a, 96), b)
    c, d = jnp.where(even, c, turn(d, 32)), jnp.where(even, turn(c, 96), d)
    return a, b, c, d


def tile(ref, i):
    return ref[:, 128 * i : 128 * i + 128]


def set_tile(ref, i, value):
    ref[:, 128 * i : 128 * i + 128] = value


def pack(field_ref, pack_ref):
    for q in range(3):
        for to, value in enumerate(swap([tile(field_ref, 4 * q + r) for r in range(4)])):
            pack_ref[to, 96 * q : 96 * q + 96, :] = value


def unpack(came_ref, field_ref):
    for q in range(3):
        for r, value in enumerate(swap([came_ref[j, 96 * q : 96 * q + 96, :] for j in range(4)])):
            set_tile(field_ref, 4 * q + r, value)


def first_nodes(field_ref, layer_ref, edge_ref):
    lane = lanes_of(K)
    edge = jnp.zeros((K, 128), F32)
    for q in range(3):
        layer = jnp.zeros((K, 128), F32)
        for r in range(4):
            value = tile(field_ref, 4 * q + r)
            layer = jnp.where(lane // 32 == r, turn(value, 32 * r), layer)
            edge = jnp.where(lane % 32 == 4 * q + r, turn(value, 4 * q + r), edge)
        layer_ref[96 * q : 96 * q + 96, :] = layer
    edge_ref[...] = edge


def put(columns_ref, field_ref, layer_ref, edge, far_edge, top):
    lane = lanes_of(K)
    for q in range(3):
        for r in range(4):
            i = 4 * q + r
            near = tile(field_ref, i)
            ahead = jnp.where(top, 0.0, turn(layer_ref[96 * q : 96 * q + 96, :], 32 * (3 - r)))
            far = jnp.where(lane < 96, turn(near, 96), ahead)
            for da, (value, side) in enumerate(((near, edge), (far, far_edge))):
                at = 8 * r + 3 * da + q
                columns_ref[pl.ds(at, K, stride=64), :] = value
                moved = jnp.where(lane % 32 == 31, turn(side, 31 - i), turn(value, 127))
                columns_ref[pl.ds(32 + at, K, stride=64), :] = moved


def far_edges(edge, corner, top):
    lane = lanes_of(K)
    corner = jnp.where(top, 0.0, jnp.where(lane < 96, 0.0, turn(corner, 96)))
    return corner, jnp.where(lane < 96, turn(edge, 96), corner)


def products(columns_ref, image_ref, stencil_ref, coef):
    weights = stencil_ref[...]
    coef = [jnp.broadcast_to(coef[r : r + 1], (8, 128)) for r in range(3)]
    wide = 8

    def step(group, carry):
        base = pl.multiple_of(64 * wide * group, 64 * wide)
        some = columns_ref[pl.ds(base, 64 * wide), :]
        high, middle, low = split(jnp.concatenate([some[64 * c : 64 * c + 64] for c in range(wide)], 1))
        stack = jnp.concatenate([high, middle, low, high, middle, high], 0)
        terms = jnp.dot(weights, stack, preferred_element_type=F32)
        for c in range(wide):
            term = terms[:, 128 * c : 128 * c + 128]

            def part(dr, r, dh):
                at = 8 * ((dr * 3 + r) * 2 + dh)
                return term[at : at + 8] * coef[r]

            values = []
            for dh in range(2):
                for node in range(4):
                    parts = [part(dr, node - dr, dh) for dr in range(2) if 0 <= node - dr < 3]
                    values.append(parts[0] if len(parts) == 1 else parts[0] + parts[1])
            image_ref[pl.ds(base + 64 * c, 64), :] = jnp.concatenate(values, 0)
        return carry

    lax.fori_loop(0, K // wide, step, 0, unroll=UNROLL)


def take(image_ref, wide_ref):
    lane = lanes_of(K)
    over, far_over = jnp.zeros((K, 128), F32), jnp.zeros((K, 128), F32)
    for q in range(3):
        layer = jnp.zeros((K, 128), F32)
        for r in range(4):
            i = 4 * q + r
            at = 8 * r + q

            def shifted_sum(at):
                second = image_ref[pl.ds(32 + at, K, stride=64), :]
                first = image_ref[pl.ds(at, K, stride=64), :]
                return first + jnp.where(lane % 32 == 0, 0.0, turn(second, 1)), turn(second, i - 31)

            near, out = shifted_sum(at)
            far, far_out = shifted_sum(at + 3)
            over = jnp.where(lane % 32 == i, out, over)
            far_over = jnp.where(lane % 32 == i, far_out, far_over)
            set_tile(wide_ref, i, near + jnp.where(lane < 32, 0.0, turn(far, 32)))
            layer = jnp.where(lane // 32 == r, turn(far, 32 * (r - 3)), layer)
        set_tile(wide_ref, 12 + q, layer)
    set_tile(wide_ref, 15, over + jnp.where(lane < 32, 0.0, turn(far_over, 32)))
    set_tile(wide_ref, 16, jnp.where(lane < 96, 0.0, far_over))


def front_kernel(
    start_hbm, search_hbm, held_hbm, ids_hbm, kmat_hbm, ritz_hbm, moduli_hbm,
    whole_hbm, whole_2_hbm, hold_hbm, s_hbm, r_hbm, p_hbm,
    s_out, r_out, p_out,
    start_in, search_in, held_ref, ids_ref, kmat_ref, ritz_row, moduli_ref, ritz_ref, stencil_ref, s, r, p, image_s, columns, image, wide, wide_s, early, late, hold,
    s_pack, p_pack, r_pack, s_came, p_came, r_came,
    s_layer, r_layer, p_layer, s_edge, r_edge, p_edge,
    s_ahead, r_ahead, p_ahead, s_side, r_side, p_side, s_corner, r_corner, p_corner,
    back, back_over, back_corner, back_came, over_came, corner_came,
    g, from_core, half, from_plane, from_z, whole,
    g_2, from_core_2, half_2, from_plane_2, from_z_2, whole_2,
    local, send, recv,
):
    axial, hoop = lax.axis_index("axial"), lax.axis_index("hoop")
    z, x = axial // 4, axial % 4
    y, core = hoop // 2, hoop % 2
    top, bottom = z == 3, z == 0
    lane = lanes_of(K)

    def at(z, x, y, core):
        return (z * 4 + x, y * 2 + core)

    def around(dz, ds):
        sector = (hoop * 4 + x + ds + 32) % 32
        return ((z + dz + 4) % 4 * 4 + sector % 4, sector // 4)

    peers = {
        "core": [at(z, x, y, 1 - core)],
        "plane": [at(z, (x + dx) % 4, (y + dy) % 4, core) for dx, dy in PLANE],
        "z": [at((z + d) % 4, x, y, core) for d in (1, 2, 3)],
        "hoop": [around(0, 1), around(0, -1), around(1, 1), around(-1, -1)],
    }
    pairs = (
        (start_hbm, start_in), (search_hbm, search_in), (held_hbm, held_ref), (ids_hbm, ids_ref),
        (kmat_hbm, kmat_ref), (ritz_hbm, ritz_row), (moduli_hbm, moduli_ref),
    )
    loads = [pltpu.make_async_copy(source, target, local.at[n]) for n, (source, target) in enumerate(pairs)]
    for load in loads:
        load.start()
    barrier = pltpu.get_barrier_semaphore()
    count = 0
    for group in peers.values():
        for peer in group:
            pl.semaphore_signal(barrier, inc=1, device_id=peer, device_id_type=MESH)
            count += 1
    used = [0]

    def copy(source, target, peer):
        index = used[0]
        used[0] += 1
        made = pltpu.make_async_remote_copy(
            src_ref=source, dst_ref=target, send_sem=send.at[index], recv_sem=recv.at[index],
            device_id=peer, device_id_type=MESH,
        )
        made.start()
        return made

    def finish(copies):
        for made in copies:
            made.wait()

    def exchange(pack_ref, came_ref):
        copies = []
        for d in (2, 1, 3):
            copies.append(copy(pack_ref.at[(x + d) % 4], came_ref.at[x], at(z, (x + d) % 4, y, core)))
        return copies

    def forward(layer, edge, ahead, side, corner):
        return [
            copy(layer, ahead, around(-1, 0)),
            copy(edge, side, around(0, -1)),
            copy(edge, corner, around(-1, -1)),
        ]

    def summed(g, from_core, half, from_plane, from_z, whole):
        copies = [copy(g.at[pl.ds((1 - core) * 32, 32)], from_core, peers["core"][0])]
        yield
        finish(copies)
        half[...] = g[pl.ds(core * 32, 32)] + from_core[...]
        copies = []
        for n, ((dx, dy), peer) in enumerate(zip(PLANE, peers["plane"])):
            part = ((x + dx) % 4 * 4 + (y + dy) % 4) * 2
            copies.append(copy(half.at[pl.ds(part, 2)], from_plane.at[n], peer))
        yield
        finish(copies)
        parts = [half[pl.ds((x * 4 + y) * 2, 2)]] + [from_plane[n] for n in range(15)]
        while len(parts) > 1:
            parts = [parts[n] + parts[n + 1] for n in range(0, len(parts), 2)]
        from_z[z] = parts[0]
        copies = [copy(from_z.at[z], from_z.at[z], peer) for peer in peers["z"]]
        yield
        finish(copies)
        first = core * 32 + (x * 4 + y) * 2
        whole[pl.ds(first, 2)] = (from_z[0] + from_z[1]) + (from_z[2] + from_z[3])
        part = whole.at[pl.ds(first, 2)]
        copies = [copy(part, part, peer) for peer in peers["plane"]]
        yield
        finish(copies)
        part = whole.at[pl.ds(core * 32, 32)]
        copies = [copy(part, part, peers["core"][0])]
        yield
        finish(copies)

    for load in loads[2:]:
        load.wait()
    coef = []
    for layer in range(3):
        ids = ids_ref[layer]
        total = jnp.zeros((1, 128), F32)
        for material in range(3):
            total = total + jnp.where(ids == material, moduli_ref[0:1, material : material + 1], 0.0)
        coef.append(total)
    free = [(1 - held_ref[node]).astype(F32) for node in range(4)]
    ritz = jnp.broadcast_to(jnp.concatenate([ritz_row[...], jnp.zeros((1, 32), F32)], 1), (K, 128))
    ritz_ref[...] = jnp.sum(jnp.where(lane == lax.broadcasted_iota(jnp.int32, (K, 128), 0), ritz, 0.0), 1, keepdims=True)
    row = lax.broadcasted_iota(jnp.int32, (8, 128), 0)
    notes = []
    for node in range(4):
        note = jnp.where(row == 0, free[node], 0.0)
        notes.append(jnp.where(row == 1, coef[node], note) if node < 3 else note)
    for to, value in enumerate(swap(notes)):
        s_pack[to, 288:296, :] = value

    def mask_in(source, field_out):
        for i in range(12):
            set_tile(field_out, i, source[pl.ds(i, K, stride=12), :] * free[i % 4])

    loads[0].wait()
    mask_in(start_in, s_out)
    pack(s_out, s_pack)
    pl.semaphore_wait(barrier, count)
    flying = exchange(s_pack, s_came)
    s_came[x] = s_pack[x]
    stencil_ref[...] = stencil(kmat_ref[...])
    zero = jnp.zeros((K, 128), F32)
    for high in range(8):
        for low in (6, 7):
            columns[pl.ds(8 * high + low, K, stride=64), :] = zero
    loads[1].wait()
    mask_in(search_in, p_out)
    pack(p_out, p_pack)
    p_flying = exchange(p_pack, p_came)
    p_came[x] = p_pack[x]
    stores = [
        pltpu.make_async_copy(s_out, s_hbm, local.at[7]),
        pltpu.make_async_copy(p_out, p_hbm, local.at[8]),
    ]
    for store in stores:
        store.start()
    finish(flying)

    def stage(work):
        pl.when(axial >= 0)(work)

    def keep(blocks, index, value):
        blocks[index, :, 0:K] = value

    notes = swap([s_came[j, 288:296, :] for j in range(4)])
    free = [note[0:1] for note in notes]
    coef = jnp.concatenate([note[1:2] for note in notes[:3]], 0)

    @stage
    def _():
        unpack(s_came, s)
        first_nodes(s, s_layer, s_edge)

    flying = forward(s_layer, s_edge, s_ahead, s_side, s_corner)

    @stage
    def _():
        keep(early, 0, mm_nt(s[...], s[...]))

    finish(p_flying)

    @stage
    def _():
        unpack(p_came, p)
        first_nodes(p, p_layer, p_edge)

    p_flying = forward(p_layer, p_edge, p_ahead, p_side, p_corner)

    @stage
    def _():
        keep(early, 1, mm_nt(s[...], p[...]))
        keep(early, 2, mm_nt(p[...], p[...]))

    def ext(field, ahead, side, corner):
        layers = [jnp.where(top, 0.0, ahead[96 * q : 96 * q + 96, :]) for q in range(3)]
        return jnp.concatenate([field[...]] + layers + [side[...], far_edges(side[...], corner[...], top)[0]], 1)

    def operate(field, ahead, side, corner, result):
        put(columns, field, ahead, side[...], far_edges(side[...], corner[...], top)[1], top)
        products(columns, image, stencil_ref, coef)
        take(image, result)

    finish(flying)

    @stage
    def _():
        operate(s, s_ahead, s_side, s_corner, wide_s)
        for q in range(3):
            back[96 * q : 96 * q + 96, :] = tile(wide_s, 12 + q)
        back_over[...] = tile(wide_s, 15)
        back_corner[...] = tile(wide_s, 16)

    flying = [
        copy(back, back_came, around(1, 0)),
        copy(back_over, over_came, around(0, 1)),
        copy(back_corner, corner_came, around(1, 1)),
    ]

    finish(p_flying)

    @stage
    def _():
        operate(p, p_ahead, p_side, p_corner, wide)
        keep(early, 5, mm_nt(wide[...], ext(p, p_ahead, p_side, p_corner)))

    finish(flying)

    @stage
    def _():
        over = over_came[...] + jnp.where(bottom, 0.0, jnp.where(lane < 32, turn(corner_came[...], 32), 0.0))
        for q in range(3):
            below = jnp.where(bottom, 0.0, back_came[96 * q : 96 * q + 96, :])
            for node in range(4):
                i = 4 * q + node
                value = tile(wide_s, i) + jnp.where(lane < 32, turn(below, -32 * node), 0.0)
                value = (value + jnp.where(lane % 32 == 0, turn(over, -i), 0.0)) * free[node]
                set_tile(image_s, i, value)
                set_tile(r, i, value - ritz_ref[...] * tile(s, i))
        first_nodes(r, r_layer, r_edge)

    flying = forward(r_layer, r_edge, r_ahead, r_side, r_corner)

    @stage
    def _():
        keep(early, 3, mm_nt(image_s[...], s[...]))
        keep(early, 4, mm_nt(image_s[...], p[...]))
        pack_gram(early, g)

    sum_1 = summed(g, from_core, half, from_plane, from_z, whole)
    next(sum_1)

    @stage
    def _():
        keep(late, 0, mm_nt(s[...], r[...]))
        keep(late, 3, mm_nt(image_s[...], r[...]))

    next(sum_1)

    @stage
    def _():
        keep(late, 1, mm_nt(p[...], r[...]))
        keep(late, 2, mm_nt(r[...], r[...]))
        pack(r, r_pack)

    finish(flying)

    @stage
    def _():
        operate(r, r_ahead, r_side, r_corner, wide)

    next(sum_1)

    @stage
    def _():
        keep(late, 5, mm_nt(wide[...], ext(r, r_ahead, r_side, r_corner)))
        keep(late, 4, mm_nt(ext(p, p_ahead, p_side, p_corner), wide[...]))
        pack_gram(late, g_2)

    sum_2 = summed(g_2, from_core_2, half_2, from_plane_2, from_z_2, whole_2)
    next(sum_2)
    next(sum_1)
    next(sum_2)
    next(sum_1)
    next(sum_2)
    r_flying = exchange(r_pack, r_came)
    r_came[x] = r_pack[x]
    next(sum_1, None)

    @stage
    def _():
        b11, _, _, a11, _, _ = unpack_gram(whole)
        d1, e1 = diagonal(a11 + b11)
        hold[0] = sweep((a11 + b11) * d1 * e1)

    next(sum_2)

    @stage
    def _():
        b11, b12, b22, a11, a12, a22 = unpack_gram(whole)
        (d1, e1), (d2, e2) = diagonal(a11 + b11), diagonal(a22 + b22)
        z1 = mm(cut(hold[0]), jnp.concatenate([(a12 + b12) * d1 * e2, b11 * d1], 1))
        s2 = jnp.concatenate([(a22 + b22) * d2 * e2, pad(cut(b12).T) * d2], 1) - mm(cut(z1).T, z1)
        hold[1], hold[2] = z1[:, :128], z1[:, 128:]
        hold[3] = sweep(s2[:, :128])
        hold[4] = s2[:, 128:]

    next(sum_2)

    @stage
    def _():
        y2 = mm(cut(hold[3]), hold[4])
        u2 = mm(cut(hold[3]).T, y2)
        hold[4], hold[5] = y2, u2
        hold[6] = mm(cut(hold[0]).T, hold[2] - mm(cut(hold[1]), u2))

    next(sum_2, None)
    finish(r_flying)

    @stage
    def _():
        unpack(r_came, r_out)

    for n, (source, target) in enumerate(((r_out, r_hbm), (whole, whole_hbm), (whole_2, whole_2_hbm))):
        stores.append(pltpu.make_async_copy(source, target, local.at[9 + n]))
        stores[-1].start()

    @stage
    def _():
        b11, _, b22, a11, _, a22 = unpack_gram(whole)
        b13, b23, b33, a13, a23, a33 = unpack_gram(whole_2)
        d1, d2, (d3, e3) = diagonal(a11 + b11)[0], diagonal(a22 + b22)[0], diagonal(a33 + b33)
        z13 = mm(cut(hold[0]), (a13 + b13) * d1 * e3)
        z23 = mm(cut(hold[3]), (a23 + b23) * d2 * e3 - mm(cut(hold[1]).T, z13))
        z3 = jnp.concatenate([z13, z23], 0)
        s3 = jnp.concatenate([(a33 + b33) * d3 * e3, pad(cut(b13).T) * d3], 1) - mm(
            cut(z3).T, jnp.concatenate([z3, jnp.concatenate([hold[2], hold[4]], 0)], 1)
        )
        hold[7], hold[8], hold[9], hold[10] = z13, z23, s3[:, :128], s3[:, 128:]

    stores.append(pltpu.make_async_copy(hold, hold_hbm, local.at[12]))
    stores[-1].start()
    for store in stores:
        store.wait()


def front(start, search, held, ids, kmat, ritz, moduli):
    def rows(*shape):
        return pltpu.VMEM(shape + (128,), F32)

    field = pltpu.VMEM((K, 1536), F32)
    return pl.pallas_call(
        front_kernel,
        out_shape=[jax.ShapeDtypeStruct(shape, F32) for shape in [(64, 8, 128)] * 2 + [(11, K, 128)] + [(K, 1536)] * 3],
        in_specs=[HBM] * 7,
        out_specs=[HBM] * 6,
        scratch_shapes=[field] * 3
        + [rows(1152)] * 2
        + [pltpu.VMEM((n, 1, 128), jnp.int32) for n in (4, 3)]
        + [pltpu.VMEM(shape, F32) for shape in ((24, 24), (1, K), (1, 3), (K, 1))]
        + [pltpu.VMEM((96, 384), BF16)]
        + [field] * 4
        + [rows(K * 64)] * 2
        + [pltpu.VMEM((K, 17 * 128), F32)] * 2
        + [rows(6, K)] * 2 + [rows(11, K)]
        + [rows(4, 296), rows(4, 288), rows(4, 288)] * 2
        + [rows(288)] * 3 + [rows(K)] * 3
        + [rows(288)] * 3 + [rows(K)] * 6
        + [rows(288), rows(K), rows(K)] * 2
        + [rows(64, 8), rows(32, 8), rows(32, 8), rows(15, 2, 8), rows(4, 2, 8), rows(64, 8)] * 2
        + [pltpu.SemaphoreType.DMA((13,)), pltpu.SemaphoreType.DMA((COPIES,)), pltpu.SemaphoreType.DMA((COPIES,))],
        compiler_params=pltpu.CompilerParams(vmem_limit_bytes=ROOM, collective_id=0, has_side_effects=True),
        name="front",
    )(start, search, held, ids, kmat, ritz, moduli)


def pack_gram(blocks, g):
    lane = lanes_of(K)
    for unit, index in enumerate((0, 1, 2, 4, 5)):
        beside = turn(blocks[3], 96 - 32 * unit) if unit < 3 else 0.0
        g[12 * unit : 12 * unit + 12] = jnp.where(lane < K, blocks[index], beside).reshape(12, 8, 128)
    g[60:64] = jnp.zeros((4, 8, 128), F32)


def unpack_gram(g):
    lane = lanes_of(K)
    units = [g[12 * unit : 12 * unit + 12].reshape(K, 128) for unit in range(5)]
    fourth = jnp.zeros((K, 128), F32)
    for n in range(3):
        fourth = jnp.where(lane // 32 == n, turn(units[n], 32 + 32 * n), fourth)
    units = [jnp.where(lane < K, unit, 0.0) for unit in units]
    return units[:3] + [fourth] + units[3:]


def rotate_kernel(
    whole_hbm, whole_2_hbm, hold_hbm, s_hbm, r_hbm, p_hbm, block_ref, search_ref,
    whole, whole_2, hold, s_ref, r_ref, p_ref, rot_ref, local,
):
    pairs = (
        (hold_hbm, hold), (whole_hbm, whole), (whole_2_hbm, whole_2),
        (s_hbm, s_ref), (r_hbm, r_ref), (p_hbm, p_ref),
    )
    loads = [pltpu.make_async_copy(source, target, local.at[n]) for n, (source, target) in enumerate(pairs)]
    for load in loads:
        load.start()
    for load in loads[:3]:
        load.wait()
    lane = lanes_of(K)
    b11, b12, b22, a11, _, a22 = unpack_gram(whole)
    b13, b23, b33, _, _, a33 = unpack_gram(whole_2)
    d1, d2, d3 = (diagonal(total)[0] for total in (a11 + b11, a22 + b22, a33 + b33))
    v3 = cut(sweep(hold[9]))
    u = jnp.concatenate([hold[6] * d1, hold[5] * d2], 0)
    h2 = mm(cut(hold[3]).T, hold[8])
    h1 = mm(cut(hold[0]).T, hold[7] - mm(cut(hold[1]), h2))
    own = jnp.where(lane == lax.broadcasted_iota(jnp.int32, (K, 128), 0), d3, 0.0)
    h = jnp.concatenate([h1 * -d1, h2 * -d2, own], 0)
    big = jnp.concatenate(
        [
            jnp.concatenate([cut(b11), cut(b12), cut(b13)], 1),
            jnp.concatenate([cut(b12).T, cut(b22), cut(b23)], 1),
            jnp.concatenate([cut(b13).T, cut(b23).T, cut(b33)], 1),
        ],
        0,
    )
    image_u = mm(big[:, : 2 * K], u)
    both = mm(cut(h).T, jnp.concatenate([image_u, mm(big, h)], 1))
    p0, p1, p2 = mm(cut(u).T, image_u[: 2 * K]), both[:, :128], cut(both[:, 128:])
    w3 = mm(v3.T, mm(v3, hold[10]))
    small = p0 + mm(cut(p1).T, w3) + mm(cut(w3).T, p1 + mm(p2, w3))
    wt = cut(jnp.concatenate([u, jnp.zeros((K, 128), F32)], 0) + mm(cut(h), w3)).T
    ds, es = diagonal(small)
    rot_ref[...] = mm(cut(sweep(small * ds * es) * es), wt) * math.sqrt(UNKNOWNS)
    rot = rot_ref[...]
    for load in loads[3:]:
        load.wait()
    for i in range(6):
        lanes = slice(256 * i, 256 * i + 256)
        tail = mm(rot[:, K:], jnp.concatenate([p_ref[:, lanes], r_ref[:, lanes]], 0))
        head = tail + mm(rot[:, :K], s_ref[:, lanes])
        for h in range(2):
            block_ref[pl.ds(2 * i + h, K, stride=12), :] = head[:, 128 * h : 128 * h + 128]
            search_ref[pl.ds(2 * i + h, K, stride=12), :] = tail[:, 128 * h : 128 * h + 128]


def rotate(*parts):
    return pl.pallas_call(
        rotate_kernel,
        out_shape=[jax.ShapeDtypeStruct((1152, 128), F32)] * 2,
        in_specs=[HBM] * 6,
        out_specs=[VMEM] * 2,
        scratch_shapes=[pltpu.VMEM((64, 8, 128), F32)] * 2
        + [pltpu.VMEM((11, K, 128), F32)]
        + [pltpu.VMEM((K, 1536), F32)] * 3
        + [pltpu.VMEM((K, 288), F32), pltpu.SemaphoreType.DMA((6,))],
        compiler_params=pltpu.CompilerParams(vmem_limit_bytes=ROOM),
        name="rotate",
    )(*parts)


def on_device(start_block, search_block, ritz_values, element_matrix, moduli, material_ids, held):
    shape = start_block.shape
    parts = front(
        start_block.reshape(1152, 128), search_block.reshape(1152, 128), held,
        material_ids, element_matrix, ritz_values.reshape(1, K), moduli.reshape(1, 3),
    )
    block, search = rotate(*parts)
    return block.reshape(shape), search.reshape(shape)


def solution(mesh):
    split_field = P(None, None, None, "axial", "hoop")
    split_nodes = P(None, "axial", "hoop")
    in_specs = (split_field, split_field, P(), P(), P(), split_nodes, split_nodes)
    return jax.shard_map(
        on_device, mesh=mesh, in_specs=in_specs, out_specs=(split_field, split_field), check_vma=False
    )
```
